128 devices in a mesh: head: 8 (over y_hi, z), inner: 4 (over y_lo, core), outer: 4 (over x).
Axes of the slice: x: 4, y: 4 (y_hi: 2, y_lo: 2; y = y_hi * 2 + y_lo), z: 4, core: 2. Of those that a mesh axis runs over, the one named last changes fastest.
Arguments:
- queries: bfloat16 [16384, 2048], P(('head', 'inner', 'outer')), may hold values from -18 to 18
- keys: bfloat16 [16384, 1024], P(('head', 'inner', 'outer')), may hold values from -6 to 6
- values: bfloat16 [16384, 1024], P(('head', 'inner', 'outer')), may hold values from -6 to 6
- output: bfloat16 [16384, 2048], P(('head', 'inner', 'outer')), may hold values from -6 to 6
- grad_output: bfloat16 [16384, 2048], P(('head', 'inner', 'outer')), may hold values from -6 to 6
- positions: int32 [16384], P(('head', 'inner', 'outer')), may hold values from 0 to 16383, as said below
Outputs:
- grad_queries: bfloat16 [16384, 2048], P(('head', 'inner', 'outer'))
- grad_keys: bfloat16 [16384, 1024], P(('head', 'inner', 'outer'))
- grad_values: bfloat16 [16384, 1024], P(('head', 'inner', 'outer'))
The draws below stay inside these ranges and needn't reach their ends.
Inputs may be any that keep to these rules, and one draw needn't show every extreme that they name: positions form a permutation of 0 to 16383.
All inputs are finite; a program needn't handle non-finite values.
Results may differ from the reference program's by a relative error of at most 0.0049.
Values may be sent and summed in bfloat16 or wider, within the bound.
A program may use at most 64 MiB of HBM per device.

```python
import jax
import jax.numpy as jnp
from jax import lax

TOK_CTX = 1024
HD = 128
QH_DEV = 2
CTX = 16
BLOCK = 128
SEQ = 16384
KV_HEADS = 8
HQ = 16


def draw_positions(key, part):
    key = jax.random.fold_in(key, 7)
    order = jax.random.permutation(key, CTX)
    row_ids = jnp.arange(SEQ, dtype=jnp.int32)
    head_idx = row_ids // (CTX * BLOCK)
    ctx_place = row_ids // BLOCK % CTX
    within = row_ids % BLOCK
    local_row = head_idx * BLOCK + within
    half_rows = TOK_CTX // 2
    picked = order[ctx_place].astype(jnp.int32)
    piece_id = jnp.where(local_row < half_rows, picked, 2 * CTX - 1 - picked)
    return (piece_id * half_rows + local_row % half_rows).astype(jnp.int32)


def block_scale(rng, shape, pieces, least, largest):
    factor_of, own = 1.0, jax.random.fold_in(rng, 6)
    for dim, parts in pieces:
        heights = jnp.exp(jax.random.uniform(jax.random.fold_in(own, dim), (parts,), jnp.float32, least / len(pieces), largest / len(pieces)))
        factor_of = factor_of * jnp.repeat(heights, shape[dim] // parts).reshape([-1 if axis == dim else 1 for axis in range(len(shape))])
    return factor_of


def normal_values(stream_key, shape, spread, limit, shards=(), kind=jnp.bfloat16):
    drawn = jax.random.normal(stream_key, shape, jnp.float32) * spread
    if len(shards) > 0:
        drawn = block_scale(stream_key, shape, shards, -0.22, 0.18) * drawn
    return jnp.clip(drawn, min=-limit, max=limit).astype(kind)


def setup_inputs(seed: int = 0) -> dict:
    key_list = jax.random.split(jax.random.key(seed), 7)
    return {
        "queries": normal_values(key_list[0], (SEQ, HQ * HD), 3.0, 18.0, ((0, 128),)),
        "keys": normal_values(key_list[1], (SEQ, KV_HEADS * HD), 1.0, 6.0, ((0, 128),)),
        "values": normal_values(key_list[2], (SEQ, KV_HEADS * HD), 1.0, 6.0, ((0, 128),)),
        "output": normal_values(key_list[3], (SEQ, HQ * HD), 1.0, 6.0, ((0, 128),)),
        "grad_output": normal_values(key_list[4], (SEQ, HQ * HD), 1.0, 6.0, ((0, 128),)),
        "positions": draw_positions(jax.random.fold_in(key_list[6], 71), 0),
    }


soft_cap = 50.0
query_scale = 1.0 / 12.0


def capped(query_tile, key_tile):
    raw_scores = jnp.einsum("qed,kd->eqk", query_tile.astype(jnp.float32), key_tile.astype(jnp.float32))
    tanh_part = jnp.tanh(raw_scores * (query_scale / soft_cap))
    return soft_cap * tanh_part, tanh_part


def reference(queries, keys, values, output, grad_output, positions):
    seq_len = queries.shape[0]
    groups = keys.shape[1] // HD
    delta_rows = jnp.sum((grad_output.astype(jnp.float32) * output.astype(jnp.float32)).reshape(seq_len, groups, QH_DEV, HD), axis=3)
    query_heads = queries.reshape(seq_len, groups, QH_DEV, HD).transpose(1, 0, 2, 3)
    dout_heads = grad_output.reshape(seq_len, groups, QH_DEV, HD).transpose(1, 0, 2, 3)
    key_heads = keys.reshape(seq_len, groups, HD).transpose(1, 0, 2)
    value_heads = values.reshape(seq_len, groups, HD).transpose(1, 0, 2)
    delta_heads = delta_rows.transpose(1, 0, 2)
    tile_rows = min(512, seq_len)
    tile_count = seq_len // tile_rows

    def per_group(head_items):
        query_group, dout_group, key_group, value_group, delta_group = head_items

        def per_tile(carry, tile_idx):
            key_grad, value_grad = carry
            offset = tile_idx * tile_rows
            query_tile = lax.dynamic_slice_in_dim(query_group, offset, tile_rows, 0)
            dout_tile = lax.dynamic_slice_in_dim(dout_group, offset, tile_rows, 0)
            delta_tile = lax.dynamic_slice_in_dim(delta_group, offset, tile_rows, 0)
            query_pos = lax.dynamic_slice_in_dim(positions, offset, tile_rows, 0)
            scores, tanh_part = capped(query_tile, key_group)
            causal = (positions[None, :] <= query_pos[:, None])[None]
            log_sums = jnp.log(jnp.sum(jnp.where(causal, jnp.exp(scores), 0.0), axis=2))
            weights = jnp.where(causal, jnp.exp(scores - log_sums[:, :, None]), 0.0)
            weights_low = weights.astype(jnp.bfloat16)
            value_grad = value_grad + jnp.einsum("eqk,qed->kd", weights_low.astype(jnp.float32), dout_tile.astype(jnp.float32))
            grad_weights = jnp.einsum("qed,kd->eqk", dout_tile.astype(jnp.float32), value_group.astype(jnp.float32))
            grad_scores = (weights * (grad_weights - delta_tile.T[:, :, None]) * (1.0 - tanh_part * tanh_part) * query_scale).astype(jnp.bfloat16)
            query_grad = jnp.einsum("eqk,kd->qed", grad_scores.astype(jnp.float32), key_group.astype(jnp.float32)).astype(jnp.bfloat16)
            key_grad = key_grad + jnp.einsum("eqk,qed->kd", grad_scores.astype(jnp.float32), query_tile.astype(jnp.float32))
            return (key_grad, value_grad), query_grad

        zero_grad = jnp.zeros((seq_len, HD), jnp.float32)
        (key_grad, value_grad), query_grad = lax.scan(per_tile, (zero_grad, zero_grad), jnp.arange(tile_count, dtype=jnp.int32))
        return query_grad.reshape(seq_len, QH_DEV, HD), key_grad.astype(jnp.bfloat16), value_grad.astype(jnp.bfloat16)

    query_grad, key_grad, value_grad = lax.map(per_group, (query_heads, dout_heads, key_heads, value_heads, delta_heads))
    grad_queries = query_grad.transpose(1, 0, 2, 3).reshape(seq_len, groups * QH_DEV * HD)
    grad_keys = key_grad.transpose(1, 0, 2).reshape(seq_len, groups * HD)
    grad_values = value_grad.transpose(1, 0, 2).reshape(seq_len, groups * HD)
    return (grad_queries, grad_keys, grad_values)
```

```python
import functools, math
import jax, jax.numpy as jnp
from jax import lax
from jax.experimental import pallas as pl
from jax.experimental.pallas import tpu as pltpu
from jax.sharding import PartitionSpec as P

f32, bf16 = jnp.float32, jnp.bfloat16
HD = 128
TILE = 512
SCALE = 1.0 / 600.0
CAP2 = 50.0 * math.log2(math.e)

def nt(a, b):
    return lax.dot_general(a, b, (((1,), (1,)), ((), ())), preferred_element_type=f32)

def nn(a, b):
    return lax.dot_general(a, b, (((1,), (0,)), ((), ())), preferred_element_type=f32)

def totals_kernel(nr, nk, span_ref, q_ref, k_ref, qpos_ref, kpos_ref, z_ref):
    z_ref[...] = jnp.zeros_like(z_ref)

    def tile(rb, kb, masked):
        rows = pl.ds(pl.multiple_of(rb * TILE, TILE), TILE)
        kk = k_ref[pl.ds(pl.multiple_of(kb * TILE, TILE), TILE), :]
        if masked:
            live = kpos_ref[pl.ds(pl.multiple_of(kb * TILE, TILE), TILE), :] <= qpos_ref[rb]
        for h in range(2):
            s = nt(kk, q_ref[rows, h * HD:(h + 1) * HD])
            e = jnp.exp2(jnp.tanh(s * SCALE) * CAP2)
            if masked:
                e = jnp.where(live, e, 0.0)
            z_ref[rb, h] += jnp.sum(e.reshape(TILE // 8, 8, TILE), axis=0)

    def step(i, _):
        rb, kb = i // nk, i % nk
        some = span_ref[2, kb] <= span_ref[1, rb]
        whole = span_ref[3, kb] <= span_ref[0, rb]
        pl.when(whole)(lambda: tile(rb, kb, False))
        pl.when(jnp.logical_and(some, jnp.logical_not(whole)))(lambda: tile(rb, kb, True))
        return 0

    lax.fori_loop(0, nr * nk, step, 0)

def totals(span, q, k, qpos, kpos):
    nr, nk = q.shape[0] // TILE, k.shape[0] // TILE
    vm = pl.BlockSpec(memory_space=pltpu.VMEM)
    return pl.pallas_call(
        functools.partial(totals_kernel, nr, nk),
        out_shape=jax.ShapeDtypeStruct((nr, 2, 8, TILE), f32),
        in_specs=[pl.BlockSpec(memory_space=pltpu.SMEM), vm, vm, vm, vm],
        out_specs=vm,
        compiler_params=pltpu.CompilerParams(vmem_limit_bytes=56 * 2**20),
        cost_estimate=pl.CostEstimate(flops=10**10, bytes_accessed=4 * 2**20, transcendentals=3 * 10**7),
        name="totals",
    )(span, q, k, qpos.reshape(nr, 1, TILE), kpos.reshape(-1, 1))

def grads_kernel(nr, nk, span_ref, q_ref, do_ref, k_ref, v_ref, z_ref, d_ref, qpos_ref, kpos_ref,
                 dq_ref, dk_ref, dv_ref, qt, dot, dq, dkt, dvt, lcol, dcol):
    dq[...] = jnp.zeros_like(dq)
    dkt[...] = jnp.zeros_like(dkt)
    dvt[...] = jnp.zeros_like(dvt)

    def prep(rb, _):
        rows = pl.ds(pl.multiple_of(rb * TILE, TILE), TILE)
        for h in range(2):
            cols = slice(h * HD, (h + 1) * HD)
            qt[rb, h] = q_ref[rows, cols].T
            dot[rb, h] = do_ref[rows, cols].T
            lz = jnp.log2(z_ref[rb, h:h + 1, :])
            lcol[rb, h] = jnp.broadcast_to(lz, (HD, TILE)).T
            dcol[rb, h] = jnp.broadcast_to(d_ref[rb, h:h + 1, :], (HD, TILE)).T
        return 0

    lax.fori_loop(0, nr, prep, 0)

    def tile(rb, kb, masked):
        rows = pl.ds(pl.multiple_of(rb * TILE, TILE), TILE)
        keys = pl.ds(pl.multiple_of(kb * TILE, TILE), TILE)
        kk = k_ref[keys, :]
        vv = v_ref[keys, :]
        if masked:
            live = kpos_ref[kb] <= qpos_ref[rows, :]
        for h in range(2):
            cols = slice(h * HD, (h + 1) * HD)
            s = nt(q_ref[rows, cols], kk)
            dp = nt(do_ref[rows, cols], vv)
            lc = jnp.concatenate([lcol[rb, h]] * (TILE // HD), axis=1)
            dc = jnp.concatenate([dcol[rb, h]] * (TILE // HD), axis=1)
            t = jnp.tanh(s * SCALE)
            w = jnp.exp2(t * CAP2 - lc)
            if masked:
                w = jnp.where(live, w, 0.0)
            g = w * (dp - dc) * (1.0 - t * t)
            wl = w.astype(bf16)
            gl = g.astype(bf16)
            dvt[kb] += nn(dot[rb, h], wl)
            dkt[kb] += nn(qt[rb, h], gl)
            dq[rb, h] += nn(gl, kk)

    def step(i, _):
        rb, kb = i // nk, i % nk
        some = span_ref[2, kb] <= span_ref[1, rb]
        whole = span_ref[3, kb] <= span_ref[0, rb]
        pl.when(whole)(lambda: tile(rb, kb, False))
        pl.when(jnp.logical_and(some, jnp.logical_not(whole)))(lambda: tile(rb, kb, True))
        return 0

    lax.fori_loop(0, nr * nk, step, 0)

    def out_rows(rb, _):
        rows = pl.ds(pl.multiple_of(rb * TILE, TILE), TILE)
        for h in range(2):
            dq_ref[rows, h * HD:(h + 1) * HD] = (dq[rb, h] * (1.0 / 12.0)).astype(bf16)
        return 0

    def out_keys(kb, _):
        keys = pl.ds(pl.multiple_of(kb * TILE, TILE), TILE)
        dk_ref[keys, :] = (dkt[kb] * (1.0 / 12.0)).T.astype(bf16)
        dv_ref[keys, :] = dvt[kb].T.astype(bf16)
        return 0

    lax.fori_loop(0, nr, out_rows, 0)
    lax.fori_loop(0, nk, out_keys, 0)

def grads(span, q, do, k, v, z, d, qpos, kpos):
    nr, nk = q.shape[0] // TILE, k.shape[0] // TILE
    vm = pl.BlockSpec(memory_space=pltpu.VMEM)
    return pl.pallas_call(
        functools.partial(grads_kernel, nr, nk),
        out_shape=(jax.ShapeDtypeStruct(q.shape, bf16), jax.ShapeDtypeStruct(k.shape, bf16), jax.ShapeDtypeStruct(k.shape, bf16)),
        in_specs=[pl.BlockSpec(memory_space=pltpu.SMEM)] + [vm] * 8,
        out_specs=(vm,) * 3,
        scratch_shapes=[
            pltpu.VMEM((nr, 2, HD, TILE), bf16), pltpu.VMEM((nr, 2, HD, TILE), bf16),
            pltpu.VMEM((nr, 2, TILE, HD), f32),
            pltpu.VMEM((nk, HD, TILE), f32), pltpu.VMEM((nk, HD, TILE), f32),
            pltpu.VMEM((nr, 2, TILE, HD), f32), pltpu.VMEM((nr, 2, TILE, HD), f32),
        ],
        compiler_params=pltpu.CompilerParams(vmem_limit_bytes=56 * 2**20),
        cost_estimate=pl.CostEstimate(flops=5 * 10**10, bytes_accessed=16 * 2**20, transcendentals=3 * 10**7),
        name="grads",
    )(span, q, do, k, v, z, d, qpos.reshape(-1, 1), kpos.reshape(nk, 1, TILE))

def spans(qpos, kpos):
    qb, kb = qpos.reshape(-1, TILE), kpos.reshape(-1, TILE)
    return jnp.stack([qb.min(1), qb.max(1), kb.min(1), kb.max(1)])


MESH = pl.DeviceIdType.MESH
HEADS, INNER, OUTER, BLK, CTX_ROWS = 8, 4, 4, 128, 1024


def peers():
    head, inner, outer = (lax.axis_index(a) for a in ("head", "inner", "outer"))
    y_peer = lax.rem(inner + 2, INNER)
    core_peer = inner + 1 - 2 * lax.rem(inner, 2)
    x_next, x_prev = lax.rem(outer + 1, OUTER), lax.rem(outer + OUTER - 1, OUTER)
    return head, inner, outer, y_peer, core_peer, x_next, x_prev


def greet(devices):
    barrier = pltpu.get_barrier_semaphore()
    for device in devices:
        pl.semaphore_signal(barrier, inc=1, device_id=device, device_id_type=MESH)
    pl.semaphore_wait(barrier, len(devices))


def rows_at(ref, block, chunk):
    return ref.at[pl.ds(pl.multiple_of(block * CTX_ROWS + chunk * BLK, BLK), BLK)]


def spread_kernel(q, do, k, v, aux, q_all, do_all, k_all, v_all, aux_r, aux_k,
                  send1, recv1, send2, recv2, own_sem):
    head, inner, outer, y_peer, core_peer, x_next, x_prev = peers()
    greet([{"head": lax.rem(head + j, HEADS)} for j in range(1, HEADS)]
          + [{"inner": y_peer}, {"inner": core_peer}, {"outer": x_next}, {"outer": x_prev}])

    def aux_at(ref, block, chunk):
        return ref.at[block, chunk]

    def first(t, dest, source_head):
        if t == 4:
            return aux.at[dest], aux_at(aux_r, inner, source_head)
        src = (q, do, k, v)[t]
        dst = (q_all, do_all, k_all, v_all)[t]
        wide = 256 if t < 2 else 128
        return (src.at[:, pl.ds(pl.multiple_of(dest * wide, wide), wide)],
                rows_at(dst, inner if t < 2 else outer, source_head))

    def remote(src, dst, ssem, rsem, device):
        return pltpu.make_async_remote_copy(src_ref=src, dst_ref=dst, send_sem=ssem, recv_sem=rsem,
                                            device_id=device, device_id_type=MESH)

    ORDER = (0, 2, 4, 3, 1)
    for t in ORDER:
        src, dst = first(t, head, head)
        pltpu.make_async_copy(src, dst, own_sem.at[t]).start()

    def send_first(j, _):
        dest = lax.rem(head + j, HEADS)
        for t in ORDER:
            src, dst = first(t, dest, head)
            remote(src, dst, send1.at[t, dest], recv1.at[t, head], {"head": dest}).start()
        return 0

    lax.fori_loop(1, HEADS, send_first, 0)
    for t in ORDER:
        src, dst = first(t, head, head)
        pltpu.make_async_copy(src, dst, own_sem.at[t]).wait()

    def piece(t, block, chunk):
        if t == 4:
            return aux_at(aux_r, block, chunk)
        if t == 5:
            return aux_at(aux_k, block, chunk)
        return rows_at((q_all, do_all, k_all, v_all)[t], block, chunk)

    ROWS, KEYS = (0, 4, 1), (2, 5, 3)

    def hop(route, t, block, chunk, device):
        ref = piece(t, block, chunk)
        s = (ROWS if t in ROWS else KEYS).index(t)
        return remote(ref, ref, send2.at[route, s, chunk], recv2.at[route, s, chunk], device)

    def aux_hop(route, chunk, device):
        return remote(aux_at(aux_r, inner, chunk), aux_at(aux_k, outer, chunk),
                      send2.at[route, 1, chunk], recv2.at[route, 1, chunk], device)

    Y, C, XN, XP = {"inner": y_peer}, {"inner": core_peer}, {"outer": x_next}, {"outer": x_prev}

    def forward(j, _):
        chunk = lax.rem(head + HEADS - j, HEADS)

        @pl.when(j > 0)
        def _():
            for t in ORDER:
                src, dst = first(t, head, chunk)
                remote(src, dst, send1.at[t, chunk], recv1.at[t, chunk], {"head": chunk}).wait_recv()

        own = pltpu.make_async_copy(aux_at(aux_r, inner, chunk), aux_at(aux_k, outer, chunk), own_sem.at[5])
        own.start()
        for t in ROWS:
            hop(0, t, inner, chunk, Y).start()
            hop(1, t, inner, chunk, C).start()
        for t in KEYS:
            if t == 5:
                aux_hop(3, chunk, XN).start()
                aux_hop(4, chunk, XP).start()
            else:
                hop(3, t, outer, chunk, XN).start()
                hop(4, t, outer, chunk, XP).start()
        own.wait()
        return 0

    lax.fori_loop(0, HEADS, forward, 0)

    def relay(j, _):
        chunk = lax.rem(head + HEADS - j, HEADS)
        for t in ROWS:
            hop(0, t, y_peer, chunk, Y).wait_recv()
            hop(2, t, y_peer, chunk, C).start()
        even = lax.rem(chunk, 2) == 0
        for t in KEYS:
            hop(3, t, x_prev, chunk, XN).wait_recv()

            @pl.when(even)
            def _():
                hop(5, t, x_prev, chunk, XN).start()

            hop(4, t, x_next, chunk, XP).wait_recv()

            @pl.when(jnp.logical_not(even))
            def _():
                hop(5, t, x_next, chunk, XP).start()
        return 0

    lax.fori_loop(0, HEADS, relay, 0)
    y_core = lax.rem(core_peer + 2, INNER)
    x_far = lax.rem(outer + 2, OUTER)

    def finish(j, _):
        chunk = lax.rem(head + HEADS - j, HEADS)
        for t in ROWS:
            hop(1, t, core_peer, chunk, C).wait_recv()
            hop(2, t, y_core, chunk, C).wait_recv()
            hop(0, t, inner, chunk, Y).wait_send()
            hop(1, t, inner, chunk, C).wait_send()
            hop(2, t, y_peer, chunk, C).wait_send()
        for t in KEYS:
            hop(5, t, x_far, chunk, XN).wait_recv()
            hop(3, t, outer, chunk, XN).wait_send()
            hop(4, t, outer, chunk, XP).wait_send()
            hop(5, t, x_prev, chunk, XN).wait_send()

        @pl.when(j > 0)
        def _():
            for t in ORDER:
                src, dst = first(t, chunk, head)
                remote(src, dst, send1.at[t, chunk], recv1.at[t, chunk], {"head": chunk}).wait_send()
        return 0

    lax.fori_loop(0, HEADS, finish, 0)


def spread(q, do, k, v, aux):
    hbm = pl.BlockSpec(memory_space=pl.ANY)
    rows = INNER * CTX_ROWS
    return pl.pallas_call(
        spread_kernel,
        out_shape=(jax.ShapeDtypeStruct((rows, 256), bf16), jax.ShapeDtypeStruct((rows, 256), bf16),
                   jax.ShapeDtypeStruct((rows, 128), bf16), jax.ShapeDtypeStruct((rows, 128), bf16),
                   jax.ShapeDtypeStruct((INNER, HEADS, 8, 128), f32), jax.ShapeDtypeStruct((OUTER, HEADS, 8, 128), f32)),
        in_specs=[hbm] * 5,
        out_specs=(hbm,) * 6,
        scratch_shapes=[pltpu.SemaphoreType.DMA((5, HEADS)), pltpu.SemaphoreType.DMA((5, HEADS)),
                        pltpu.SemaphoreType.DMA((6, 3, HEADS)), pltpu.SemaphoreType.DMA((6, 3, HEADS)),
                        pltpu.SemaphoreType.DMA((6,))],
        compiler_params=pltpu.CompilerParams(collective_id=0, has_side_effects=True),
        name="spread",
    )(q, do, k, v, aux)


def pool_kernel(z, out, recv, send_sem, recv_sem):
    head, inner, outer, y_peer, core_peer, x_next, x_prev = peers()
    others = [lax.rem(inner + j, INNER) for j in range(1, INNER)]
    greet([{"inner": o} for o in others])
    out[...] = jnp.sum(z[...], axis=2)
    copies = []
    for j, o in enumerate(others):
        copies.append(pltpu.make_async_remote_copy(
            src_ref=out, dst_ref=recv.at[j], send_sem=send_sem.at[j], recv_sem=recv_sem.at[j],
            device_id={"inner": o}, device_id_type=MESH))
        copies[-1].start()
    for c in copies:
        c.wait()
    total = jnp.zeros(out.shape, f32)
    for i in range(INNER):
        d = lax.rem(inner - i + INNER, INNER)
        part = jnp.where(d == 0, out[...], jnp.where(d == 1, recv[0], jnp.where(d == 2, recv[1], recv[2])))
        total = total + part
    out[...] = total


def pool(z):
    vm = pl.BlockSpec(memory_space=pltpu.VMEM)
    small = (z.shape[0], 2, z.shape[3])
    return pl.pallas_call(
        pool_kernel,
        out_shape=jax.ShapeDtypeStruct(small, f32),
        in_specs=[vm], out_specs=vm,
        scratch_shapes=[pltpu.VMEM((3,) + small, f32), pltpu.SemaphoreType.DMA((3,)), pltpu.SemaphoreType.DMA((3,))],
        compiler_params=pltpu.CompilerParams(collective_id=1, has_side_effects=True),
        name="pool",
    )(z)


def collect_kernel(dq, dk, dv, gq, gk, gv, dq_pair, dq_sum, dq_far, kv_far, low_q, low_k, low_v,
                   send_sem, recv_sem, send_out, recv_out, own_sem):
    head, inner, outer, y_peer, core_peer, x_next, x_prev = peers()
    x_far = lax.rem(outer + 2, OUTER)
    greet([{"head": lax.rem(head + j, HEADS)} for j in range(1, HEADS)]
          + [{"inner": y_peer}, {"inner": core_peer}, {"outer": x_next}, {"outer": x_prev}, {"outer": x_far}])
    y_core = lax.rem(core_peer + 2, INNER)
    Y, C = {"inner": y_peer}, {"inner": core_peer}
    XS = ({"outer": x_next}, {"outer": x_far}, {"outer": x_prev})
    XI = (x_next, x_far, x_prev)

    def remote(src, dst, ssem, rsem, device):
        return pltpu.make_async_remote_copy(src_ref=src, dst_ref=dst, send_sem=ssem, recv_sem=rsem,
                                            device_id=device, device_id_type=MESH)

    def local_rows(chunk):
        return pl.ds(pl.multiple_of(chunk * BLK, BLK), BLK)

    def pair_copy(which, chunk):
        block = core_peer if which == 0 else y_core
        return remote(rows_at(dq, block, chunk), dq_pair.at[which, local_rows(chunk)],
                      send_sem.at[which, chunk], recv_sem.at[which, chunk], C)

    def far_copy(chunk):
        return remote(dq_sum.at[local_rows(chunk)], dq_far.at[local_rows(chunk)],
                      send_sem.at[2, chunk], recv_sem.at[2, chunk], Y)

    def kv_copy(t, x, chunk):
        n = 3 + 3 * t + x
        return remote(rows_at((dk, dv)[t], XI[x], chunk), kv_far.at[t, x, local_rows(chunk)],
                      send_sem.at[n, chunk], recv_sem.at[n, chunk], XS[x])

    def out_copy(t, chunk):
        low, out, wide = ((low_q, gq, 256), (low_k, gk, 128), (low_v, gv, 128))[t]
        return remote(low.at[local_rows(chunk)], out.at[:, pl.ds(pl.multiple_of(head * wide, wide), wide)],
                      send_out.at[t, chunk], recv_out.at[t, head], {"head": chunk})

    def chunk_at(j):
        return lax.rem(head + 1 + j, HEADS)

    def send_pair(j, _):
        chunk = chunk_at(j)
        pair_copy(0, chunk).start()
        pair_copy(1, chunk).start()
        for t in range(2):
            for x in range(3):
                kv_copy(t, x, chunk).start()
        return 0

    lax.fori_loop(0, HEADS, send_pair, 0)

    def block_rows(block, chunk):
        return pl.ds(pl.multiple_of(block * CTX_ROWS + chunk * BLK, BLK), BLK)

    def sum_pair(j, _):
        chunk = chunk_at(j)
        pair_copy(0, chunk).wait_recv()
        pair_copy(1, chunk).wait_recv()
        rows = local_rows(chunk)
        dq_sum[rows, :] = (dq[block_rows(y_peer, chunk), :].astype(f32) + dq_pair[1, rows, :].astype(f32)).astype(bf16)
        far_copy(chunk).start()
        return 0

    lax.fori_loop(0, HEADS, sum_pair, 0)

    def sum_all(j, _):
        chunk = chunk_at(j)
        rows = local_rows(chunk)
        for t in range(2):
            for x in range(3):
                kv_copy(t, x, chunk).wait_recv()
            src, low = ((dk, low_k), (dv, low_v))[t]
            total = src[block_rows(outer, chunk), :].astype(f32)
            for x in range(3):
                total = total + kv_far[t, x, rows, :].astype(f32)
            low[rows, :] = total.astype(bf16)
        far_copy(chunk).wait_recv()
        low_q[rows, :] = (dq[block_rows(inner, chunk), :].astype(f32) + dq_pair[0, rows, :].astype(f32)
                          + dq_far[rows, :].astype(f32)).astype(bf16)

        @pl.when(j < HEADS - 1)
        def _():
            for t in range(3):
                out_copy(t, chunk).start()
        return 0

    lax.fori_loop(0, HEADS, sum_all, 0)
    own = []
    for t in range(3):
        low, out, wide = ((low_q, gq, 256), (low_k, gk, 128), (low_v, gv, 128))[t]
        own.append(pltpu.make_async_copy(low.at[local_rows(head)],
                                         out.at[:, pl.ds(pl.multiple_of(head * wide, wide), wide)], own_sem.at[t]))
        own[-1].start()

    def finish(j, _):
        chunk = chunk_at(j)
        for which in range(2):
            pair_copy(which, chunk).wait_send()
        far_copy(chunk).wait_send()
        for t in range(2):
            for x in range(3):
                kv_copy(t, x, chunk).wait_send()

        @pl.when(j < HEADS - 1)
        def _():
            for t in range(3):
                low, out, wide = ((low_q, gq, 256), (low_k, gk, 128), (low_v, gv, 128))[t]
                out_copy(t, chunk).wait_send()
                remote(low.at[local_rows(head)], out.at[:, pl.ds(pl.multiple_of(chunk * wide, wide), wide)],
                       send_out.at[t, head], recv_out.at[t, chunk], {"head": chunk}).wait_recv()
        return 0

    lax.fori_loop(0, HEADS, finish, 0)
    for copy in own:
        copy.wait()


def collect(dq, dk, dv):
    vm = pl.BlockSpec(memory_space=pltpu.VMEM)
    hbm = pl.BlockSpec(memory_space=pl.ANY)
    return pl.pallas_call(
        collect_kernel,
        out_shape=(jax.ShapeDtypeStruct((BLK, 2048), bf16), jax.ShapeDtypeStruct((BLK, 1024), bf16),
                   jax.ShapeDtypeStruct((BLK, 1024), bf16)),
        in_specs=[vm] * 3,
        out_specs=(hbm,) * 3,
        scratch_shapes=[pltpu.VMEM((2, CTX_ROWS, 256), bf16), pltpu.VMEM((CTX_ROWS, 256), bf16),
                        pltpu.VMEM((CTX_ROWS, 256), bf16), pltpu.VMEM((2, 3, CTX_ROWS, 128), bf16),
                        pltpu.VMEM((CTX_ROWS, 256), bf16), pltpu.VMEM((CTX_ROWS, 128), bf16),
                        pltpu.VMEM((CTX_ROWS, 128), bf16),
                        pltpu.SemaphoreType.DMA((9, HEADS)), pltpu.SemaphoreType.DMA((9, HEADS)),
                        pltpu.SemaphoreType.DMA((3, HEADS)), pltpu.SemaphoreType.DMA((3, HEADS)),
                        pltpu.SemaphoreType.DMA((3,))],
        compiler_params=pltpu.CompilerParams(collective_id=2, has_side_effects=True, vmem_limit_bytes=40 * 2**20),
        name="collect",
    )(dq, dk, dv)


def local(queries, keys, values, output, grad_output, positions):
    delta = jnp.sum((grad_output.astype(f32) * output.astype(f32)).reshape(BLK, HEADS, 2, HD), axis=3)
    delta = delta.transpose(1, 2, 0)
    place = jnp.broadcast_to(positions.astype(f32)[None, None, :], (HEADS, 1, BLK))
    aux = jnp.concatenate([delta, place, jnp.zeros((HEADS, 5, BLK), f32)], axis=1)
    q, do, k, v, aux_r, aux_k = spread(queries, grad_output, keys, values, aux)
    d = aux_r[:, :, 0:2, :].transpose(2, 0, 1, 3).reshape(2, -1, TILE).transpose(1, 0, 2)
    qpos = aux_r[:, :, 2, :].reshape(-1).astype(jnp.int32)
    kpos = aux_k[:, :, 2, :].reshape(-1).astype(jnp.int32)
    span = spans(qpos, kpos)
    z = pool(totals(span, q, k, qpos, kpos))
    dq, dk, dv = grads(span, q, do, k, v, z, d, qpos, kpos)
    return collect(dq, dk, dv)


def solution(mesh):
    rows = P(("head", "inner", "outer"), None)
    return jax.shard_map(
        local, mesh=mesh,
        in_specs=(rows,) * 5 + (P(("head", "inner", "outer")),),
        out_specs=(rows,) * 3,
        check_vma=False,
    )
```

```python
import functools, math
import jax, jax.numpy as jnp
from jax import lax
from jax.experimental import pallas as pl
from jax.experimental.pallas import tpu as pltpu
from jax.sharding import PartitionSpec as P

f32, bf16 = jnp.float32, jnp.bfloat16
HD = 128
TILE = 512
STRIP = 256
SCALE = 1.0 / 600.0
CAP2 = 50.0 * math.log2(math.e)

def nt(a, b):
    return lax.dot_general(a, b, (((1,), (1,)), ((), ())), preferred_element_type=f32)

def nn(a, b):
    return lax.dot_general(a, b, (((1,), (0,)), ((), ())), preferred_element_type=f32)

def place_of(aux, block):
    part = aux[block // 2, pl.ds(pl.multiple_of(lax.rem(block, 2) * 4, 4), 4), 2:3, :]
    return jnp.concatenate([part[c] for c in range(4)], axis=1)


def delta_of(aux, block, h):
    part = aux[block // 2, pl.ds(pl.multiple_of(lax.rem(block, 2) * 4, 4), 4), h:h + 1, :]
    return jnp.concatenate([part[c] for c in range(4)], axis=1)


def column(row):
    return jnp.broadcast_to(row, (HD, TILE)).T


def widen(col):
    return jnp.concatenate([col] * (TILE // HD), axis=1)


WHOLE, PARTLY = 0, 4096


def live_tiles(nr, nk, aux_r, aux_k, span, tiles):
    for b in range(nr):
        part = aux_r[b // 2, 4 * (b % 2):4 * (b % 2) + 4, 2, :]
        span[0, b] = jnp.min(part)
        span[1, b] = jnp.max(part)
    for b in range(nk):
        part = aux_k[b // 2, 4 * (b % 2):4 * (b % 2) + 4, 2, :]
        span[2, b] = jnp.min(part)
        span[3, b] = jnp.max(part)
    tiles[1] = nr * 64 + nk

    def scan(i, n):
        kb, rb = i // nr, lax.rem(i, nr)
        some = span[2, kb] <= span[1, rb]
        whole = span[3, kb] <= span[0, rb]

        @pl.when(some)
        def _():
            tiles[n + 2] = jnp.where(whole, WHOLE, PARTLY) + rb * 64 + kb
        return n + some.astype(jnp.int32)

    n = lax.fori_loop(0, nr * nk, scan, 0)
    tiles[0] = n
    tiles[n + 2] = nr * 64 + nk


def totals_kernel(nr, nk, q_ref, k_ref, aux_r, aux_k, z_ref, tiles, span):
    z_ref[...] = jnp.zeros_like(z_ref)
    live_tiles(nr, nk, aux_r, aux_k, span, tiles)

    def tile(rb, kb, masked):
        rows = pl.ds(pl.multiple_of(rb * TILE, TILE), TILE)
        kk = k_ref[pl.ds(pl.multiple_of(kb * TILE, TILE), TILE), :]
        if masked:
            live = widen(column(place_of(aux_k, kb))) <= place_of(aux_r, rb)
        for h in range(2):
            s = nt(kk, q_ref[rows, h * HD:(h + 1) * HD])
            e = jnp.exp2(jnp.tanh(s * SCALE) * CAP2)
            if masked:
                e = jnp.where(live, e, 0.0)
            z_ref[rb, h] += jnp.sum(e.reshape(TILE // 8, 8, TILE), axis=0)

    def step(i, _):
        code = tiles[i + 2]
        rb, kb = (code // 64) % 64, code % 64
        pl.when(code < PARTLY)(lambda: tile(rb, kb, False))
        pl.when(code >= PARTLY)(lambda: tile(rb, kb, True))
        return 0

    lax.fori_loop(0, tiles[0], step, 0)


def totals(q, k, aux_r, aux_k):
    nr, nk = q.shape[0] // TILE, k.shape[0] // TILE
    vm = pl.BlockSpec(memory_space=pltpu.VMEM)
    return pl.pallas_call(
        functools.partial(totals_kernel, nr, nk),
        out_shape=(jax.ShapeDtypeStruct((nr, 2, 8, TILE), f32), jax.ShapeDtypeStruct((nr * nk + 8,), jnp.int32)),
        in_specs=[vm, vm, vm, vm],
        out_specs=(vm, pl.BlockSpec(memory_space=pltpu.SMEM)),
        scratch_shapes=[pltpu.SMEM((4, 8), f32)],
        compiler_params=pltpu.CompilerParams(vmem_limit_bytes=60 * 2**20),
        cost_estimate=pl.CostEstimate(flops=2 * 10**10, bytes_accessed=4 * 2**20, transcendentals=3 * 10**7),
        name="totals",
    )(q, k, aux_r, aux_k)


def grads_kernel(nr, nk, tiles, q_ref, do_ref, k_ref, v_ref, z_ref, aux_r, aux_k,
                 dq_ref, dk_ref, dv_ref, qs, dos, qt, dot, dq, dkt, dvt, lcol, dcol, wbuf, gbuf):
    dq[...] = jnp.zeros_like(dq)
    dkt[...] = jnp.zeros_like(dkt)
    dvt[...] = jnp.zeros_like(dvt)

    def prep(rb, _):
        rows = pl.ds(pl.multiple_of(rb * TILE, TILE), TILE)
        for h in range(2):
            cols = slice(h * HD, (h + 1) * HD)
            hr = slice(h * TILE, (h + 1) * TILE)
            qs[rb, hr, :] = q_ref[rows, cols]
            dos[rb, hr, :] = do_ref[rows, cols]
            qt[rb, :, hr] = q_ref[rows, cols].T
            dot[rb, :, hr] = do_ref[rows, cols].T
            lcol[rb, hr, :] = column(jnp.log2(z_ref[rb, h:h + 1, :]))
            dcol[rb, hr, :] = column(delta_of(aux_r, rb, h))
        return 0

    lax.fori_loop(0, nr, prep, 0)

    def keys_of(ref, kb):
        return ref[pl.ds(pl.multiple_of(kb * TILE, TILE), TILE), :]

    def body(i, masked):
        now, last = tiles[i + 2], tiles[i + 1]
        rc, kc = (last // 64) % 64, last % 64
        ra, ka = jnp.minimum((now // 64) % 64, nr - 1), jnp.minimum(now % 64, nk - 1)
        kk = keys_of(k_ref, ka)
        vv = keys_of(v_ref, ka)
        kcc = keys_of(k_ref, jnp.minimum(kc, nk - 1))
        if masked:
            live = place_of(aux_k, ka) <= widen(column(place_of(aux_r, ra)))
        dv_sum, dk_sum = dvt[kc], dkt[kc]
        for c in range(2 * TILE // STRIP):
            hr = slice(c * STRIP, (c + 1) * STRIP)
            w, g = wbuf[hr, :], gbuf[hr, :]
            dv_sum = dv_sum + nn(dot[rc, :, hr], w)
            dk_sum = dk_sum + nn(qt[rc, :, hr], g)
            dq[rc, hr, :] += nn(g, kcc)
            t = jnp.tanh(nt(qs[ra, hr, :], kk) * SCALE)
            p = nt(dos[ra, hr, :], vv)
            w = jnp.exp2(t * CAP2 - widen(lcol[ra, hr, :]))
            if masked:
                lo = c * STRIP % TILE
                w = jnp.where(live[lo:lo + STRIP], w, 0.0)
            g = w * (p - widen(dcol[ra, hr, :])) * (1.0 - t * t)
            wbuf[hr, :] = w.astype(bf16)
            gbuf[hr, :] = g.astype(bf16)
        dvt[kc] = dv_sum
        dkt[kc] = dk_sum

    def step(i, _):
        masked = tiles[i + 2] >= PARTLY
        pl.when(jnp.logical_not(masked))(lambda: body(i, False))
        pl.when(masked)(lambda: body(i, True))
        return 0

    lax.fori_loop(0, tiles[0] + 1, step, 0)

    def out_rows(rb, _):
        rows = pl.ds(pl.multiple_of(rb * TILE, TILE), TILE)
        for h in range(2):
            dq_ref[rows, h * HD:(h + 1) * HD] = (dq[rb, h * TILE:(h + 1) * TILE, :] * (1.0 / 12.0)).astype(bf16)
        return 0

    def out_keys(kb, _):
        keys = pl.ds(pl.multiple_of(kb * TILE, TILE), TILE)
        dk_ref[keys, :] = (dkt[kb] * (1.0 / 12.0)).T.astype(bf16)
        dv_ref[keys, :] = dvt[kb].T.astype(bf16)
        return 0

    lax.fori_loop(0, nr, out_rows, 0)
    lax.fori_loop(0, nk, out_keys, 0)


def grads(tiles, q, do, k, v, z, aux_r, aux_k):
    nr, nk = q.shape[0] // TILE, k.shape[0] // TILE
    vm = pl.BlockSpec(memory_space=pltpu.VMEM)
    return pl.pallas_call(
        functools.partial(grads_kernel, nr, nk),
        out_shape=(jax.ShapeDtypeStruct(q.shape, bf16), jax.ShapeDtypeStruct(k.shape, bf16), jax.ShapeDtypeStruct(k.shape, bf16)),
        in_specs=[pl.BlockSpec(memory_space=pltpu.SMEM)] + [vm] * 7,
        out_specs=(vm,) * 3,
        scratch_shapes=[
            pltpu.VMEM((nr, 2 * TILE, HD), bf16), pltpu.VMEM((nr, 2 * TILE, HD), bf16),
            pltpu.VMEM((nr + 1, HD, 2 * TILE), bf16), pltpu.VMEM((nr + 1, HD, 2 * TILE), bf16),
            pltpu.VMEM((nr + 1, 2 * TILE, HD), f32),
            pltpu.VMEM((nk + 1, HD, TILE), f32), pltpu.VMEM((nk + 1, HD, TILE), f32),
            pltpu.VMEM((nr, 2 * TILE, HD), f32), pltpu.VMEM((nr, 2 * TILE, HD), f32),
            pltpu.VMEM((2 * TILE, TILE), bf16), pltpu.VMEM((2 * TILE, TILE), bf16),
        ],
        compiler_params=pltpu.CompilerParams(vmem_limit_bytes=60 * 2**20),
        cost_estimate=pl.CostEstimate(flops=5 * 10**10, bytes_accessed=16 * 2**20, transcendentals=3 * 10**7),
        name="grads",
    )(tiles, q, do, k, v, z, aux_r, aux_k)


MESH = pl.DeviceIdType.MESH
HEADS, INNER, OUTER, BLK, CTX_ROWS = 8, 4, 4, 128, 1024


def peers():
    head, inner, outer = (lax.axis_index(a) for a in ("head", "inner", "outer"))
    y_peer = lax.rem(inner + 2, INNER)
    core_peer = inner + 1 - 2 * lax.rem(inner, 2)
    x_next, x_prev = lax.rem(outer + 1, OUTER), lax.rem(outer + OUTER - 1, OUTER)
    return head, inner, outer, y_peer, core_peer, x_next, x_prev


def neighbours():
    head, inner, outer, y_peer, core_peer, x_next, x_prev = peers()
    across = (1 - head // 4) * 4
    return ([{"head": lax.rem(head + j, HEADS)} for j in range(1, HEADS)]
            + [{"head": across + z, "inner": y_peer} for z in range(4)]
            + [{"inner": y_peer}, {"inner": core_peer}, {"outer": x_next}, {"outer": x_prev}])


def greet(devices):
    barrier = pltpu.get_barrier_semaphore()
    for device in devices:
        pl.semaphore_signal(barrier, inc=1, device_id=device, device_id_type=MESH)
    pl.semaphore_wait(barrier, len(devices))


def rows_at(ref, block, chunk):
    return ref.at[pl.ds(pl.multiple_of(block * CTX_ROWS + chunk * BLK, BLK), BLK)]


def spread_kernel(q, do, k, v, out, pos, q_all, do_all, k_all, v_all, aux_r, aux_k,
                  aux, send1, recv1, send2, recv2, own_sem):
    head, inner, outer, y_peer, core_peer, x_next, x_prev = peers()
    greet(neighbours())

    def aux_at(ref, block, chunk):
        return ref.at[block, chunk]

    def fill_aux():
        for g in range(HEADS):
            aux[g, 2:8, :] = jnp.broadcast_to(pos[...].astype(f32), (6, BLK))
            for h in range(2):
                cols = slice((2 * g + h) * HD, (2 * g + h + 1) * HD)
                product = do[:, cols].astype(f32) * out[:, cols].astype(f32)
                aux[g, h:h + 1, :] = jnp.sum(product.T, axis=0, keepdims=True)

    def near(chunk):
        return chunk // 4 == head // 4

    def via(t, dest):
        if t in (0, 1, 4):
            return {"head": dest, "inner": jnp.where(near(dest), inner, y_peer)}
        return {"head": dest}

    def first(t, dest, source_head):
        if t == 4:
            return aux.at[dest], aux_at(aux_r, inner, source_head)
        if t == 5:
            return aux.at[dest], aux_at(aux_k, outer, source_head)
        src = (q, do, k, v)[t]
        dst = (q_all, do_all, k_all, v_all)[t]
        wide = 256 if t < 2 else 128
        return (src.at[:, pl.ds(pl.multiple_of(dest * wide, wide), wide)],
                rows_at(dst, inner if t < 2 else outer, source_head))

    def remote(src, dst, ssem, rsem, device):
        return pltpu.make_async_remote_copy(src_ref=src, dst_ref=dst, send_sem=ssem, recv_sem=rsem,
                                            device_id=device, device_id_type=MESH)

    ORDER = (0, 2, 4, 5, 3, 1)
    def send_part(part):
        for t in part:
            src, dst = first(t, head, head)
            pltpu.make_async_copy(src, dst, own_sem.at[t]).start()

        def send_first(j, _):
            dest = lax.rem(head + j, HEADS)
            for t in part:
                src, dst = first(t, dest, head)
                remote(src, dst, send1.at[t, dest], recv1.at[t, head], via(t, dest)).start()
            return 0

        lax.fori_loop(1, HEADS, send_first, 0)

    EARLY, LATE = (0, 2), (1, 3, 4, 5)
    send_part(EARLY)
    fill_aux()
    send_part(LATE)
    for t in ORDER:
        src, dst = first(t, head, head)
        pltpu.make_async_copy(src, dst, own_sem.at[t]).wait()

    def piece(t, block, chunk):
        if t == 4:
            return aux_at(aux_r, block, chunk)
        if t == 5:
            return aux_at(aux_k, block, chunk)
        return rows_at((q_all, do_all, k_all, v_all)[t], block, chunk)

    ROWS, KEYS = (0, 4, 1), (2, 5, 3)

    def hop(route, t, block, chunk, device):
        ref = piece(t, block, chunk)
        s = (ROWS if t in ROWS else KEYS).index(t)
        return remote(ref, ref, send2.at[route, s, chunk], recv2.at[route, s, chunk], device)

    Y, C, XN, XP = {"inner": y_peer}, {"inner": core_peer}, {"outer": x_next}, {"outer": x_prev}

    def forward(part, j):
        chunk = lax.rem(head + HEADS - j, HEADS)

        @pl.when(j > 0)
        def _():
            for t in part:
                src, dst = first(t, head, chunk)
                remote(src, dst, send1.at[t, chunk], recv1.at[t, chunk], {"head": chunk}).wait_recv()

        block = jnp.where(near(chunk), inner, y_peer)
        for t in part:
            if t in ROWS:
                hop(0, t, block, chunk, Y).start()
                hop(1, t, block, chunk, C).start()
            else:
                hop(3, t, outer, chunk, XN).start()
                hop(4, t, outer, chunk, XP).start()

    def relay(part, j):
        chunk = lax.rem(head + HEADS - j, HEADS)
        block = jnp.where(near(chunk), y_peer, inner)
        even = lax.rem(chunk, 2) == 0
        for t in part:
            if t in ROWS:
                hop(0, t, block, chunk, Y).wait_recv()
                hop(2, t, block, chunk, C).start()
        keys = [t for t in part if t in KEYS]
        for t in keys:
            hop(3, t, x_prev, chunk, XN).wait_recv()
            hop(4, t, x_next, chunk, XP).wait_recv()

        @pl.when(even)
        def _():
            for t in keys:
                hop(5, t, x_prev, chunk, XN).start()

        @pl.when(jnp.logical_not(even))
        def _():
            for t in keys:
                hop(5, t, x_next, chunk, XP).start()

    def steps(*calls):
        def step(j, _):
            for fn, part in calls:
                fn(part, j)
            return 0
        lax.fori_loop(0, HEADS, step, 0)

    steps((forward, EARLY))
    steps((forward, LATE), (relay, EARLY))
    steps((relay, LATE))
    y_core = lax.rem(core_peer + 2, INNER)
    x_far = lax.rem(outer + 2, OUTER)

    def finish(j, _):
        chunk = lax.rem(head + HEADS - j, HEADS)
        for t in ROWS:
            hop(1, t, core_peer, chunk, C).wait_recv()
            hop(2, t, y_core, chunk, C).wait_recv()
            hop(0, t, inner, chunk, Y).wait_send()
            hop(1, t, inner, chunk, C).wait_send()
            hop(2, t, y_peer, chunk, C).wait_send()
        for t in KEYS:
            hop(5, t, x_far, chunk, XN).wait_recv()
            hop(3, t, outer, chunk, XN).wait_send()
            hop(4, t, outer, chunk, XP).wait_send()
            hop(5, t, x_prev, chunk, XN).wait_send()

        @pl.when(j > 0)
        def _():
            for t in ORDER:
                src, dst = first(t, chunk, head)
                remote(src, dst, send1.at[t, chunk], recv1.at[t, chunk], {"head": chunk}).wait_send()
        return 0

    lax.fori_loop(0, HEADS, finish, 0)


def spread(q, do, k, v, out, pos):
    hbm = pl.BlockSpec(memory_space=pl.ANY)
    vm = pl.BlockSpec(memory_space=pltpu.VMEM)
    rows = INNER * CTX_ROWS
    return pl.pallas_call(
        spread_kernel,
        out_shape=(jax.ShapeDtypeStruct((rows, 256), bf16), jax.ShapeDtypeStruct((rows, 256), bf16),
                   jax.ShapeDtypeStruct((rows, 128), bf16), jax.ShapeDtypeStruct((rows, 128), bf16),
                   jax.ShapeDtypeStruct((INNER, HEADS, 8, 128), f32), jax.ShapeDtypeStruct((OUTER, HEADS, 8, 128), f32)),
        in_specs=[hbm, vm, hbm, hbm, vm, vm],
        out_specs=(hbm,) * 6,
        scratch_shapes=[pltpu.VMEM((HEADS, 8, 128), f32),
                        pltpu.SemaphoreType.DMA((6, HEADS)), pltpu.SemaphoreType.DMA((6, HEADS)),
                        pltpu.SemaphoreType.DMA((6, 3, HEADS)), pltpu.SemaphoreType.DMA((6, 3, HEADS)),
                        pltpu.SemaphoreType.DMA((6,))],
        compiler_params=pltpu.CompilerParams(collective_id=0, has_side_effects=True, vmem_limit_bytes=60 * 2**20),
        name="spread",
    )(q, do, k, v, out, pos)


def pool_kernel(z, out, recv, send_sem, recv_sem):
    head, inner, outer, y_peer, core_peer, x_next, x_prev = peers()
    others = [lax.rem(inner + j, INNER) for j in range(1, INNER)]
    greet([{"inner": o} for o in others])
    out[...] = jnp.sum(z[...], axis=2)
    copies = []
    for j, o in enumerate(others):
        copies.append(pltpu.make_async_remote_copy(
            src_ref=out, dst_ref=recv.at[j], send_sem=send_sem.at[j], recv_sem=recv_sem.at[j],
            device_id={"inner": o}, device_id_type=MESH))
        copies[-1].start()
    for c in copies:
        c.wait()
    total = jnp.zeros(out.shape, f32)
    for i in range(INNER):
        d = lax.rem(inner - i + INNER, INNER)
        part = jnp.where(d == 0, out[...], jnp.where(d == 1, recv[0], jnp.where(d == 2, recv[1], recv[2])))
        total = total + part
    out[...] = total


def pool(z):
    vm = pl.BlockSpec(memory_space=pltpu.VMEM)
    small = (z.shape[0], 2, z.shape[3])
    return pl.pallas_call(
        pool_kernel,
        out_shape=jax.ShapeDtypeStruct(small, f32),
        in_specs=[vm], out_specs=vm,
        scratch_shapes=[pltpu.VMEM((3,) + small, f32), pltpu.SemaphoreType.DMA((3,)), pltpu.SemaphoreType.DMA((3,))],
        compiler_params=pltpu.CompilerParams(collective_id=1, has_side_effects=True),
        name="pool",
    )(z)


def collect_kernel(dq, dk, dv, gq, gk, gv, q_near, kv_near, dq_pair, dq_sum, dq_far, kv_far, kv_relay, kv_sum,
                   low_q, low_k, low_v, send_sem, recv_sem, send_out, recv_out, own_sem):
    head, inner, outer, y_peer, core_peer, x_next, x_prev = peers()
    x_far = lax.rem(outer + 2, OUTER)

    def block_rows(block):
        return pl.ds(pl.multiple_of(block * CTX_ROWS, CTX_ROWS), CTX_ROWS)

    held = [pltpu.make_async_copy(dq.at[block_rows(y_peer)], q_near.at[1], own_sem.at[0]),
            pltpu.make_async_copy(dq.at[block_rows(inner)], q_near.at[0], own_sem.at[1])]
    for t in range(2):
        for x, block in enumerate((x_next, x_prev, outer)):
            held.append(pltpu.make_async_copy((dk, dv)[t].at[block_rows(block)], kv_near.at[t, x], own_sem.at[2 + 3 * t + x]))
    for copy in held:
        copy.start()
    greet(neighbours())
    y_core = lax.rem(core_peer + 2, INNER)
    Y, C, XN, XP = {"inner": y_peer}, {"inner": core_peer}, {"outer": x_next}, {"outer": x_prev}

    def remote(src, dst, ssem, rsem, device):
        return pltpu.make_async_remote_copy(src_ref=src, dst_ref=dst, send_sem=ssem, recv_sem=rsem,
                                            device_id=device, device_id_type=MESH)

    def local_rows(chunk):
        return pl.ds(pl.multiple_of(chunk * BLK, BLK), BLK)

    def near(chunk):
        return chunk // 4 == head // 4

    def pair_copy(which, chunk):
        block = jnp.where(near(chunk), *((core_peer, y_core) if which == 0 else (y_core, core_peer)))
        return remote(rows_at(dq, block, chunk), dq_pair.at[which, local_rows(chunk)],
                      send_sem.at[which, chunk], recv_sem.at[which, chunk], C)

    def far_copy(chunk):
        return remote(dq_sum.at[local_rows(chunk)], dq_far.at[local_rows(chunk)],
                      send_sem.at[2, chunk], recv_sem.at[2, chunk], Y)

    def kv_copy(t, x, chunk, device, summed=False):
        n = 3 + 3 * t + x
        src = kv_sum.at[t, local_rows(chunk)] if summed else rows_at((dk, dv)[t], (x_next, x_prev, x_far)[x], chunk)
        dst = kv_relay.at[t, local_rows(chunk)] if x == 2 else kv_far.at[t, x, local_rows(chunk)]
        return remote(src, dst, send_sem.at[n, chunk], recv_sem.at[n, chunk], device)

    def out_copy(t, chunk):
        low, out, wide = ((low_q, gq, 256), (low_k, gk, 128), (low_v, gv, 128))[t]
        device = {"head": chunk, "inner": jnp.where(near(chunk), inner, y_peer)} if t == 0 else {"head": chunk}
        return remote(low.at[local_rows(chunk)], out.at[:, pl.ds(pl.multiple_of(head * wide, wide), wide)],
                      send_out.at[t, chunk], recv_out.at[t, head], device)

    def chunk_at(j):
        return lax.rem(head + 1 + j, HEADS)

    def send_pair(j, _):
        chunk = chunk_at(j)
        even = lax.rem(chunk, 2) == 0

        @pl.when(even)
        def _():
            for t in range(2):
                kv_copy(t, 2, chunk, XN).start()

        @pl.when(jnp.logical_not(even))
        def _():
            for t in range(2):
                kv_copy(t, 2, chunk, XP).start()

        pair_copy(1, chunk).start()
        pair_copy(0, chunk).start()

        @pl.when(even)
        def _():
            for t in range(2):
                kv_copy(t, 1, chunk, XP).start()

        @pl.when(jnp.logical_not(even))
        def _():
            for t in range(2):
                kv_copy(t, 0, chunk, XN).start()
        return 0

    lax.fori_loop(0, HEADS, send_pair, 0)
    for copy in held:
        copy.wait()

    def sum_pair(j, _):
        chunk = chunk_at(j)
        rows = local_rows(chunk)
        pair_copy(1, chunk).wait_recv()
        mine = jnp.where(near(chunk), 0, 1)
        dq_sum[rows, :] = (q_near[1 - mine, rows, :].astype(f32) + dq_pair[1, rows, :].astype(f32)).astype(bf16)
        far_copy(chunk).start()
        odd = lax.rem(chunk, 2)
        for t in range(2):
            kv_copy(t, 2, chunk, XN).wait_recv()
            kv_sum[t, rows, :] = (kv_near[t, odd, rows, :].astype(f32) + kv_relay[t, rows, :].astype(f32)).astype(bf16)

        @pl.when(odd == 0)
        def _():
            for t in range(2):
                kv_copy(t, 0, chunk, XN, True).start()

        @pl.when(odd == 1)
        def _():
            for t in range(2):
                kv_copy(t, 1, chunk, XP, True).start()
        return 0

    lax.fori_loop(0, HEADS, sum_pair, 0)

    def sum_all(j, _):
        chunk = chunk_at(j)
        rows = local_rows(chunk)
        pair_copy(0, chunk).wait_recv()
        far_copy(chunk).wait_recv()
        mine = jnp.where(near(chunk), 0, 1)
        low_q[rows, :] = (q_near[mine, rows, :].astype(f32) + dq_pair[0, rows, :].astype(f32)
                          + dq_far[rows, :].astype(f32)).astype(bf16)
        pl.when(j < HEADS - 1)(lambda: out_copy(0, chunk).start())
        for t in range(2):
            total = kv_near[t, 2, rows, :].astype(f32)
            for x in range(2):
                kv_copy(t, x, chunk, XN).wait_recv()
                total = total + kv_far[t, x, rows, :].astype(f32)
            (low_k, low_v)[t][rows, :] = total.astype(bf16)

        @pl.when(j < HEADS - 1)
        def _():
            for t in (1, 2):
                out_copy(t, chunk).start()
        return 0

    lax.fori_loop(0, HEADS, sum_all, 0)
    own = []
    for t in range(3):
        low, out, wide = ((low_q, gq, 256), (low_k, gk, 128), (low_v, gv, 128))[t]
        own.append(pltpu.make_async_copy(low.at[local_rows(head)],
                                         out.at[:, pl.ds(pl.multiple_of(head * wide, wide), wide)], own_sem.at[t]))
        own[-1].start()

    def finish(j, _):
        chunk = chunk_at(j)
        for which in range(2):
            pair_copy(which, chunk).wait_send()
        far_copy(chunk).wait_send()
        for t in range(2):
            for x in range(3):
                kv_copy(t, x, chunk, XN).wait_send()

        @pl.when(j < HEADS - 1)
        def _():
            for t in range(3):
                low, out, wide = ((low_q, gq, 256), (low_k, gk, 128), (low_v, gv, 128))[t]
                out_copy(t, chunk).wait_send()
                remote(low.at[local_rows(head)], out.at[:, pl.ds(pl.multiple_of(chunk * wide, wide), wide)],
                       send_out.at[t, head], recv_out.at[t, chunk], {"head": chunk}).wait_recv()
        return 0

    lax.fori_loop(0, HEADS, finish, 0)
    for copy in own:
        copy.wait()


def collect(dq, dk, dv):
    hbm = pl.BlockSpec(memory_space=pl.ANY)
    wide, narrow = (CTX_ROWS, 256), (CTX_ROWS, 128)
    return pl.pallas_call(
        collect_kernel,
        out_shape=(jax.ShapeDtypeStruct((BLK, 2048), bf16), jax.ShapeDtypeStruct((BLK, 1024), bf16),
                   jax.ShapeDtypeStruct((BLK, 1024), bf16)),
        in_specs=[hbm] * 3,
        out_specs=(hbm,) * 3,
        scratch_shapes=[pltpu.VMEM((2,) + wide, bf16), pltpu.VMEM((2, 3) + narrow, bf16),
                        pltpu.VMEM((2,) + wide, bf16), pltpu.VMEM(wide, bf16), pltpu.VMEM(wide, bf16),
                        pltpu.VMEM((2, 2) + narrow, bf16), pltpu.VMEM((2,) + narrow, bf16), pltpu.VMEM((2,) + narrow, bf16),
                        pltpu.VMEM(wide, bf16), pltpu.VMEM(narrow, bf16), pltpu.VMEM(narrow, bf16),
                        pltpu.SemaphoreType.DMA((9, HEADS)), pltpu.SemaphoreType.DMA((9, HEADS)),
                        pltpu.SemaphoreType.DMA((3, HEADS)), pltpu.SemaphoreType.DMA((3, HEADS)),
                        pltpu.SemaphoreType.DMA((8,))],
        compiler_params=pltpu.CompilerParams(collective_id=2, has_side_effects=True, vmem_limit_bytes=60 * 2**20),
        name="collect",
    )(dq, dk, dv)


def local(queries, keys, values, output, grad_output, positions):
    q, do, k, v, aux_r, aux_k = spread(queries, grad_output, keys, values, output, positions.reshape(1, BLK))
    z, tiles = totals(q, k, aux_r, aux_k)
    dq, dk, dv = grads(tiles, q, do, k, v, pool(z), aux_r, aux_k)
    return collect(dq, dk, dv)


def solution(mesh):
    rows = P(("head", "inner", "outer"), None)
    return jax.shard_map(
        local, mesh=mesh,
        in_specs=(rows,) * 5 + (P(("head", "inner", "outer")),),
        out_specs=(rows,) * 3,
        check_vma=False,
    )
```

```python
import functools, math
import jax, jax.numpy as jnp
from jax import lax
from jax.experimental import pallas as pl
from jax.experimental.pallas import tpu as pltpu
from jax.sharding import PartitionSpec as P

f32, bf16 = jnp.float32, jnp.bfloat16
HD = 128
TILE = 512
STRIP = 256
SCALE = 1.0 / 600.0
CAP2 = 50.0 * math.log2(math.e)

def nt(a, b):
    return lax.dot_general(a, b, (((1,), (1,)), ((), ())), preferred_element_type=f32)

def nn(a, b):
    return lax.dot_general(a, b, (((1,), (0,)), ((), ())), preferred_element_type=f32)

def place_of(aux, block):
    part = aux[block // 2, pl.ds(pl.multiple_of(lax.rem(block, 2) * 4, 4), 4), 2:3, :]
    return jnp.concatenate([part[c] for c in range(4)], axis=1)


def delta_of(aux, block, h):
    part = aux[block // 2, pl.ds(pl.multiple_of(lax.rem(block, 2) * 4, 4), 4), h:h + 1, :]
    return jnp.concatenate([part[c] for c in range(4)], axis=1)


def column(row):
    return jnp.broadcast_to(row, (HD, TILE)).T


def widen(col):
    return jnp.concatenate([col] * (TILE // HD), axis=1)


WHOLE, PARTLY = 0, 4096


def live_tiles(nr, nk, aux_r, aux_k, span, tiles, rest):
    for b in range(nr):
        part = aux_r[b // 2, 4 * (b % 2):4 * (b % 2) + 4, 2, :]
        span[0, b] = jnp.min(part)
        span[1, b] = jnp.max(part)
    for b in range(nk):
        part = aux_k[b // 2, 4 * (b % 2):4 * (b % 2) + 4, 2, :]
        span[2, b] = jnp.min(part)
        span[3, b] = jnp.max(part)
    tiles[1] = nr * 64 + nk

    def scan(i, counts):
        n, m = counts
        kb, rb = i // nr, lax.rem(i, nr)
        some = span[2, kb] <= span[1, rb]
        whole = span[3, kb] <= span[0, rb]

        @pl.when(some)
        def _():
            code = jnp.where(whole, WHOLE, PARTLY) + rb * 64 + kb
            tiles[n + 2] = code
            rest[m] = code
        step = some.astype(jnp.int32)
        made = jnp.logical_and(lax.rem(rb, 2) == 1, lax.rem(kb, 2) == 0)
        return n + step, m + jnp.where(made, 0, step)

    n, m = lax.fori_loop(0, nr * nk, scan, (0, 0))
    tiles[0] = n
    tiles[n + 2] = nr * 64 + nk
    return m


def totals_kernel(nr, nk, q_ref, k_ref, aux_r, aux_k, part_ref, z_ref, tiles, span, rest):
    for b in range(nr):
        z_ref[b] = part_ref[b // 2] if b % 2 else jnp.zeros((2, 8, TILE), f32)
    count = live_tiles(nr, nk, aux_r, aux_k, span, tiles, rest)

    def tile(rb, kb, masked):
        rows = pl.ds(pl.multiple_of(rb * TILE, TILE), TILE)
        kk = k_ref[pl.ds(pl.multiple_of(kb * TILE, TILE), TILE), :]
        if masked:
            live = widen(column(place_of(aux_k, kb))) <= place_of(aux_r, rb)
        for h in range(2):
            s = nt(kk, q_ref[rows, h * HD:(h + 1) * HD])
            e = jnp.exp2(jnp.tanh(s * SCALE) * CAP2)
            if masked:
                e = jnp.where(live, e, 0.0)
            z_ref[rb, h] += jnp.sum(e.reshape(TILE // 8, 8, TILE), axis=0)

    def step(i, _):
        code = rest[i]
        rb, kb = (code // 64) % 64, code % 64
        pl.when(code < PARTLY)(lambda: tile(rb, kb, False))
        pl.when(code >= PARTLY)(lambda: tile(rb, kb, True))
        return 0

    lax.fori_loop(0, count, step, 0)


def totals(q, k, aux_r, aux_k, part):
    nr, nk = q.shape[0] // TILE, k.shape[0] // TILE
    vm = pl.BlockSpec(memory_space=pltpu.VMEM)
    return pl.pallas_call(
        functools.partial(totals_kernel, nr, nk),
        out_shape=(jax.ShapeDtypeStruct((nr, 2, 8, TILE), f32), jax.ShapeDtypeStruct((nr * nk + 8,), jnp.int32)),
        in_specs=[vm] * 5,
        out_specs=(vm, pl.BlockSpec(memory_space=pltpu.SMEM)),
        scratch_shapes=[pltpu.SMEM((4, 8), f32), pltpu.SMEM((nr * nk + 8,), jnp.int32)],
        compiler_params=pltpu.CompilerParams(vmem_limit_bytes=60 * 2**20),
        cost_estimate=pl.CostEstimate(flops=2 * 10**10, bytes_accessed=4 * 2**20, transcendentals=3 * 10**7),
        name="totals",
    )(q, k, aux_r, aux_k, part)


def grads_kernel(nr, nk, tiles, q_ref, do_ref, k_ref, v_ref, z_ref, aux_r, aux_k,
                 dq_ref, dk_ref, dv_ref, qs, dos, qt, dot, dq, dkt, dvt, lcol, dcol, wbuf, gbuf):
    dq[...] = jnp.zeros_like(dq)
    dkt[...] = jnp.zeros_like(dkt)
    dvt[...] = jnp.zeros_like(dvt)

    def prep(rb, _):
        rows = pl.ds(pl.multiple_of(rb * TILE, TILE), TILE)
        for h in range(2):
            cols = slice(h * HD, (h + 1) * HD)
            hr = slice(h * TILE, (h + 1) * TILE)
            qs[rb, hr, :] = q_ref[rows, cols]
            dos[rb, hr, :] = do_ref[rows, cols]
            qt[rb, :, hr] = q_ref[rows, cols].T
            dot[rb, :, hr] = do_ref[rows, cols].T
            lcol[rb, hr, :] = column(jnp.log2(z_ref[rb, h:h + 1, :]))
            dcol[rb, hr, :] = column(delta_of(aux_r, rb, h))
        return 0

    lax.fori_loop(0, nr, prep, 0)

    def keys_of(ref, kb):
        return ref[pl.ds(pl.multiple_of(kb * TILE, TILE), TILE), :]

    def body(i, masked):
        now, last = tiles[i + 2], tiles[i + 1]
        rc, kc = (last // 64) % 64, last % 64
        ra, ka = jnp.minimum((now // 64) % 64, nr - 1), jnp.minimum(now % 64, nk - 1)
        kk = keys_of(k_ref, ka)
        vv = keys_of(v_ref, ka)
        kcc = keys_of(k_ref, jnp.minimum(kc, nk - 1))
        if masked:
            live = place_of(aux_k, ka) <= widen(column(place_of(aux_r, ra)))
        dv_sum, dk_sum = dvt[kc], dkt[kc]
        for c in range(2 * TILE // STRIP):
            hr = slice(c * STRIP, (c + 1) * STRIP)
            w, g = wbuf[hr, :], gbuf[hr, :]
            dv_sum = dv_sum + nn(dot[rc, :, hr], w)
            dk_sum = dk_sum + nn(qt[rc, :, hr], g)
            dq[rc, hr, :] += nn(g, kcc)
            t = jnp.tanh(nt(qs[ra, hr, :], kk) * SCALE)
            p = nt(dos[ra, hr, :], vv)
            w = jnp.exp2(t * CAP2 - widen(lcol[ra, hr, :]))
            if masked:
                lo = c * STRIP % TILE
                w = jnp.where(live[lo:lo + STRIP], w, 0.0)
            g = w * (p - widen(dcol[ra, hr, :])) * (1.0 - t * t)
            wbuf[hr, :] = w.astype(bf16)
            gbuf[hr, :] = g.astype(bf16)
        dvt[kc] = dv_sum
        dkt[kc] = dk_sum

    def step(i, _):
        masked = tiles[i + 2] >= PARTLY
        pl.when(jnp.logical_not(masked))(lambda: body(i, False))
        pl.when(masked)(lambda: body(i, True))
        return 0

    lax.fori_loop(0, tiles[0] + 1, step, 0)

    def out_rows(rb, _):
        rows = pl.ds(pl.multiple_of(rb * TILE, TILE), TILE)
        for h in range(2):
            dq_ref[rows, h * HD:(h + 1) * HD] = (dq[rb, h * TILE:(h + 1) * TILE, :] * (1.0 / 12.0)).astype(bf16)
        return 0

    def out_keys(kb, _):
        keys = pl.ds(pl.multiple_of(kb * TILE, TILE), TILE)
        dk_ref[keys, :] = (dkt[kb] * (1.0 / 12.0)).T.astype(bf16)
        dv_ref[keys, :] = dvt[kb].T.astype(bf16)
        return 0

    lax.fori_loop(0, nr, out_rows, 0)
    lax.fori_loop(0, nk, out_keys, 0)


def grads(tiles, q, do, k, v, z, aux_r, aux_k):
    nr, nk = q.shape[0] // TILE, k.shape[0] // TILE
    vm = pl.BlockSpec(memory_space=pltpu.VMEM)
    return pl.pallas_call(
        functools.partial(grads_kernel, nr, nk),
        out_shape=(jax.ShapeDtypeStruct(q.shape, bf16), jax.ShapeDtypeStruct(k.shape, bf16), jax.ShapeDtypeStruct(k.shape, bf16)),
        in_specs=[pl.BlockSpec(memory_space=pltpu.SMEM)] + [vm] * 7,
        out_specs=(vm,) * 3,
        scratch_shapes=[
            pltpu.VMEM((nr, 2 * TILE, HD), bf16), pltpu.VMEM((nr, 2 * TILE, HD), bf16),
            pltpu.VMEM((nr + 1, HD, 2 * TILE), bf16), pltpu.VMEM((nr + 1, HD, 2 * TILE), bf16),
            pltpu.VMEM((nr + 1, 2 * TILE, HD), f32),
            pltpu.VMEM((nk + 1, HD, TILE), f32), pltpu.VMEM((nk + 1, HD, TILE), f32),
            pltpu.VMEM((nr, 2 * TILE, HD), f32), pltpu.VMEM((nr, 2 * TILE, HD), f32),
            pltpu.VMEM((2 * TILE, TILE), bf16), pltpu.VMEM((2 * TILE, TILE), bf16),
        ],
        compiler_params=pltpu.CompilerParams(vmem_limit_bytes=60 * 2**20),
        cost_estimate=pl.CostEstimate(flops=5 * 10**10, bytes_accessed=16 * 2**20, transcendentals=3 * 10**7),
        name="grads",
    )(tiles, q, do, k, v, z, aux_r, aux_k)


MESH = pl.DeviceIdType.MESH
HEADS, INNER, OUTER, BLK, CTX_ROWS = 8, 4, 4, 128, 1024


def peers():
    head, inner, outer = (lax.axis_index(a) for a in ("head", "inner", "outer"))
    y_peer = lax.rem(inner + 2, INNER)
    core_peer = inner + 1 - 2 * lax.rem(inner, 2)
    x_next, x_prev = lax.rem(outer + 1, OUTER), lax.rem(outer + OUTER - 1, OUTER)
    return head, inner, outer, y_peer, core_peer, x_next, x_prev


def neighbours():
    head, inner, outer, y_peer, core_peer, x_next, x_prev = peers()
    across = (1 - head // 4) * 4
    return ([{"head": lax.rem(head + j, HEADS)} for j in range(1, HEADS)]
            + [{"head": across + z, "inner": y_peer} for z in range(4)]
            + [{"inner": y_peer}, {"inner": core_peer}, {"outer": x_next}, {"outer": x_prev}])


def greet(devices):
    barrier = pltpu.get_barrier_semaphore()
    for device in devices:
        pl.semaphore_signal(barrier, inc=1, device_id=device, device_id_type=MESH)
    pl.semaphore_wait(barrier, len(devices))


def rows_at(ref, block, chunk):
    return ref.at[pl.ds(pl.multiple_of(block * CTX_ROWS + chunk * BLK, BLK), BLK)]


def spread_kernel(q, do, k, v, out, pos, q_all, do_all, k_all, v_all, aux_r, aux_k, z_ref,
                  aux, send1, recv1, send2, recv2, own_sem):
    head, inner, outer, y_peer, core_peer, x_next, x_prev = peers()
    greet(neighbours())

    def aux_at(ref, block, chunk):
        return ref.at[block, chunk]

    def fill_aux():
        for g in range(HEADS):
            aux[g, 2:8, :] = jnp.broadcast_to(pos[...].astype(f32), (6, BLK))
            for h in range(2):
                cols = slice((2 * g + h) * HD, (2 * g + h + 1) * HD)
                product = do[:, cols].astype(f32) * out[:, cols].astype(f32)
                aux[g, h:h + 1, :] = jnp.sum(product.T, axis=0, keepdims=True)

    def near(chunk):
        return chunk // 4 == head // 4

    def via(t, dest):
        if t in (0, 1, 4):
            return {"head": dest, "inner": jnp.where(near(dest), inner, y_peer)}
        return {"head": dest}

    def first(t, dest, source_head):
        if t == 4:
            return aux.at[dest], aux_at(aux_r, inner, source_head)
        if t == 5:
            return aux.at[dest], aux_at(aux_k, outer, source_head)
        src = (q, do, k, v)[t]
        dst = (q_all, do_all, k_all, v_all)[t]
        wide = 256 if t < 2 else 128
        return (src.at[:, pl.ds(pl.multiple_of(dest * wide, wide), wide)],
                rows_at(dst, inner if t < 2 else outer, source_head))

    def remote(src, dst, ssem, rsem, device):
        return pltpu.make_async_remote_copy(src_ref=src, dst_ref=dst, send_sem=ssem, recv_sem=rsem,
                                            device_id=device, device_id_type=MESH)

    ORDER = (0, 2, 4, 5, 3, 1)
    def send_part(part):
        for t in part:
            src, dst = first(t, head, head)
            pltpu.make_async_copy(src, dst, own_sem.at[t]).start()

        def send_first(j, _):
            dest = lax.rem(head + j, HEADS)
            for t in part:
                src, dst = first(t, dest, head)
                remote(src, dst, send1.at[t, dest], recv1.at[t, head], via(t, dest)).start()
            return 0

        lax.fori_loop(1, HEADS, send_first, 0)

    EARLY, LATE = (0, 2, 4, 5), (1, 3)
    send_part((0, 2))
    fill_aux()
    send_part((4, 5))
    send_part(LATE)

    def wait_own(part):
        for t in part:
            src, dst = first(t, head, head)
            pltpu.make_async_copy(src, dst, own_sem.at[t]).wait()

    wait_own(EARLY)

    y_core = lax.rem(core_peer + 2, INNER)
    x_far = lax.rem(outer + 2, OUTER)

    def base(g):
        return 4 * (head // 4) if g == 0 else 4 * (1 - head // 4)

    def piece(t, block, g):
        if t >= 4:
            return (aux_r, aux_k)[t - 4].at[block, pl.ds(base(g), 4)]
        return (q_all, do_all, k_all, v_all)[t].at[pl.ds(pl.multiple_of(block * CTX_ROWS + base(g) * BLK, 4 * BLK), 4 * BLK)]

    ROWS, KEYS = (0, 4, 1), (2, 5, 3)

    def hop(route, t, block, g, device):
        ref = piece(t, block, g)
        s = (ROWS if t in ROWS else KEYS).index(t)
        return remote(ref, ref, send2.at[route, s, g], recv2.at[route, s, g], device)

    Y, C, XN, XP = {"inner": y_peer}, {"inner": core_peer}, {"outer": x_next}, {"outer": x_prev}

    def forward(part, g):
        def wait_first(chunk):
            for t in part:
                src, dst = first(t, head, chunk)
                remote(src, dst, send1.at[t, chunk], recv1.at[t, chunk], {"head": chunk}).wait_recv()

        for n in range(4):
            chunk = base(g) + lax.rem(head + 4 - n, 4)
            if g == 1 or n > 0:
                wait_first(chunk)
        for t in part:
            if t in ROWS:
                block = inner if g == 0 else y_peer
                hop(0, t, block, g, Y).start()
                hop(1, t, block, g, C).start()
            else:
                hop(3, t, outer, g, XN).start()
                hop(4, t, outer, g, XP).start()

    def relay(part, g):
        for t in part:
            if t in ROWS:
                block = y_peer if g == 0 else inner
                hop(0, t, block, g, Y).wait_recv()
                hop(2, t, block, g, C).start()
        for t in part:
            if t in KEYS:
                hop(3, t, x_prev, g, XN).wait_recv()
                hop(4, t, x_next, g, XP).wait_recv()
                if g == 0:
                    hop(5, t, x_prev, g, XN).start()
                else:
                    hop(5, t, x_next, g, XP).start()

    def arrive(part):
        for g in range(2):
            for t in part:
                if t in ROWS:
                    hop(1, t, core_peer, g, C).wait_recv()
                    hop(2, t, y_core, g, C).wait_recv()
                else:
                    hop(5, t, x_far, g, XN).wait_recv()

    def tile(n):
        r, c = n // 4, lax.rem(n, 4)
        live = widen(column(place_of(aux_k, 2 * c))) <= place_of(aux_r, 2 * r + 1)
        kk = k_all[pl.ds(pl.multiple_of(c * CTX_ROWS, CTX_ROWS), TILE), :]
        rows = pl.ds(pl.multiple_of(r * CTX_ROWS + TILE, TILE), TILE)
        for h in range(2):
            e = jnp.exp2(jnp.tanh(nt(kk, q_all[rows, h * HD:(h + 1) * HD]) * SCALE) * CAP2)
            z_ref[r, h] += jnp.sum(jnp.where(live, e, 0.0).reshape(TILE // 8, 8, TILE), axis=0)

    def some_tiles(start, stop):
        def step(n, _):
            tile(n)
            return 0
        lax.fori_loop(start, stop, step, 0)

    forward(EARLY, 0)
    forward(EARLY, 1)
    z_ref[...] = jnp.zeros_like(z_ref)
    wait_own(LATE)
    relay(EARLY, 0)
    forward(LATE, 0)
    relay(EARLY, 1)
    arrive(EARLY)
    some_tiles(0, 4)
    forward(LATE, 1)
    some_tiles(4, 8)
    relay(LATE, 0)
    some_tiles(8, 14)
    relay(LATE, 1)
    some_tiles(14, 16)
    arrive(LATE)

    for g in range(2):
        for t in ROWS:
            hop(0, t, inner, g, Y).wait_send()
            hop(1, t, inner, g, C).wait_send()
            hop(2, t, y_peer, g, C).wait_send()
        for t in KEYS:
            hop(3, t, outer, g, XN).wait_send()
            hop(4, t, outer, g, XP).wait_send()
            hop(5, t, x_prev, g, XN).wait_send()

    def finish(j, _):
        chunk = lax.rem(head + HEADS - j, HEADS)
        for t in ORDER:
            src, dst = first(t, chunk, head)
            remote(src, dst, send1.at[t, chunk], recv1.at[t, chunk], {"head": chunk}).wait_send()
        return 0

    lax.fori_loop(1, HEADS, finish, 0)


def spread(q, do, k, v, out, pos):
    hbm = pl.BlockSpec(memory_space=pl.ANY)
    vm = pl.BlockSpec(memory_space=pltpu.VMEM)
    rows = INNER * CTX_ROWS
    return pl.pallas_call(
        spread_kernel,
        out_shape=(jax.ShapeDtypeStruct((rows, 256), bf16), jax.ShapeDtypeStruct((rows, 256), bf16),
                   jax.ShapeDtypeStruct((rows, 128), bf16), jax.ShapeDtypeStruct((rows, 128), bf16),
                   jax.ShapeDtypeStruct((INNER, HEADS, 8, 128), f32), jax.ShapeDtypeStruct((OUTER, HEADS, 8, 128), f32),
                   jax.ShapeDtypeStruct((INNER, 2, 8, TILE), f32)),
        in_specs=[vm] * 6,
        out_specs=(vm, hbm, vm, hbm, vm, vm, vm),
        scratch_shapes=[pltpu.VMEM((HEADS, 8, 128), f32),
                        pltpu.SemaphoreType.DMA((6, HEADS)), pltpu.SemaphoreType.DMA((6, HEADS)),
                        pltpu.SemaphoreType.DMA((6, 3, 2)), pltpu.SemaphoreType.DMA((6, 3, 2)),
                        pltpu.SemaphoreType.DMA((6,))],
        compiler_params=pltpu.CompilerParams(collective_id=0, has_side_effects=True, vmem_limit_bytes=60 * 2**20),
        name="spread",
    )(q, do, k, v, out, pos)


def pool_kernel(z, out, recv, send_sem, recv_sem):
    head, inner, outer, y_peer, core_peer, x_next, x_prev = peers()
    others = [lax.rem(inner + j, INNER) for j in range(1, INNER)]
    greet([{"inner": o} for o in others])
    out[...] = jnp.sum(z[...], axis=2)
    copies = []
    for j, o in enumerate(others):
        copies.append(pltpu.make_async_remote_copy(
            src_ref=out, dst_ref=recv.at[j], send_sem=send_sem.at[j], recv_sem=recv_sem.at[j],
            device_id={"inner": o}, device_id_type=MESH))
        copies[-1].start()
    for c in copies:
        c.wait()
    total = jnp.zeros(out.shape, f32)
    for i in range(INNER):
        d = lax.rem(inner - i + INNER, INNER)
        part = jnp.where(d == 0, out[...], jnp.where(d == 1, recv[0], jnp.where(d == 2, recv[1], recv[2])))
        total = total + part
    out[...] = total


def pool(z):
    vm = pl.BlockSpec(memory_space=pltpu.VMEM)
    small = (z.shape[0], 2, z.shape[3])
    return pl.pallas_call(
        pool_kernel,
        out_shape=jax.ShapeDtypeStruct(small, f32),
        in_specs=[vm], out_specs=vm,
        scratch_shapes=[pltpu.VMEM((3,) + small, f32), pltpu.SemaphoreType.DMA((3,)), pltpu.SemaphoreType.DMA((3,))],
        compiler_params=pltpu.CompilerParams(collective_id=1, has_side_effects=True),
        name="pool",
    )(z)


def collect_kernel(dq, dk, dv, gq, gk, gv, q_near, kv_near, dq_pair, dq_sum, dq_far, kv_far, kv_relay, kv_sum,
                   low_q, low_k, low_v, send_sem, recv_sem, send_out, recv_out, own_sem):
    head, inner, outer, y_peer, core_peer, x_next, x_prev = peers()
    x_far = lax.rem(outer + 2, OUTER)

    def block_rows(block):
        return pl.ds(pl.multiple_of(block * CTX_ROWS, CTX_ROWS), CTX_ROWS)

    held = [pltpu.make_async_copy(dq.at[block_rows(y_peer)], q_near.at[1], own_sem.at[0]),
            pltpu.make_async_copy(dq.at[block_rows(inner)], q_near.at[0], own_sem.at[1])]
    for t in range(2):
        for x, block in enumerate((x_next, x_prev, outer)):
            held.append(pltpu.make_async_copy((dk, dv)[t].at[block_rows(block)], kv_near.at[t, x], own_sem.at[2 + 3 * t + x]))
    for copy in held:
        copy.start()
    greet(neighbours())
    y_core = lax.rem(core_peer + 2, INNER)
    Y, C, XN, XP = {"inner": y_peer}, {"inner": core_peer}, {"outer": x_next}, {"outer": x_prev}

    def remote(src, dst, ssem, rsem, device):
        return pltpu.make_async_remote_copy(src_ref=src, dst_ref=dst, send_sem=ssem, recv_sem=rsem,
                                            device_id=device, device_id_type=MESH)

    def local_rows(chunk):
        return pl.ds(pl.multiple_of(chunk * BLK, BLK), BLK)

    def near(chunk):
        return chunk // 4 == head // 4

    def pair_copy(which, chunk):
        block = jnp.where(near(chunk), *((core_peer, y_core) if which == 0 else (y_core, core_peer)))
        return remote(rows_at(dq, block, chunk), dq_pair.at[which, local_rows(chunk)],
                      send_sem.at[which, chunk], recv_sem.at[which, chunk], C)

    def far_copy(chunk):
        return remote(dq_sum.at[local_rows(chunk)], dq_far.at[local_rows(chunk)],
                      send_sem.at[2, chunk], recv_sem.at[2, chunk], Y)

    def kv_copy(t, x, chunk, device, summed=False):
        n = 3 + 3 * t + x
        src = kv_sum.at[t, local_rows(chunk)] if summed else rows_at((dk, dv)[t], (x_next, x_prev, x_far)[x], chunk)
        dst = kv_relay.at[t, local_rows(chunk)] if x == 2 else kv_far.at[t, x, local_rows(chunk)]
        return remote(src, dst, send_sem.at[n, chunk], recv_sem.at[n, chunk], device)

    def out_copy(t, chunk):
        low, out, wide = ((low_q, gq, 256), (low_k, gk, 128), (low_v, gv, 128))[t]
        device = {"head": chunk, "inner": jnp.where(near(chunk), inner, y_peer)} if t == 0 else {"head": chunk}
        return remote(low.at[local_rows(chunk)], out.at[:, pl.ds(pl.multiple_of(head * wide, wide), wide)],
                      send_out.at[t, chunk], recv_out.at[t, head], device)

    def chunk_at(j):
        return lax.rem(head + 1 + j, HEADS)

    def send_pair(j, _):
        chunk = chunk_at(j)
        even = lax.rem(chunk, 2) == 0

        @pl.when(even)
        def _():
            for t in range(2):
                kv_copy(t, 2, chunk, XN).start()

        @pl.when(jnp.logical_not(even))
        def _():
            for t in range(2):
                kv_copy(t, 2, chunk, XP).start()

        pair_copy(1, chunk).start()
        pair_copy(0, chunk).start()

        @pl.when(even)
        def _():
            for t in range(2):
                kv_copy(t, 1, chunk, XP).start()

        @pl.when(jnp.logical_not(even))
        def _():
            for t in range(2):
                kv_copy(t, 0, chunk, XN).start()
        return 0

    lax.fori_loop(0, HEADS, send_pair, 0)
    for copy in held:
        copy.wait()

    def sum_pair(j, _):
        chunk = chunk_at(j)
        rows = local_rows(chunk)
        pair_copy(1, chunk).wait_recv()
        mine = jnp.where(near(chunk), 0, 1)
        dq_sum[rows, :] = (q_near[1 - mine, rows, :].astype(f32) + dq_pair[1, rows, :].astype(f32)).astype(bf16)
        far_copy(chunk).start()
        odd = lax.rem(chunk, 2)
        for t in range(2):
            kv_copy(t, 2, chunk, XN).wait_recv()
            kv_sum[t, rows, :] = (kv_near[t, odd, rows, :].astype(f32) + kv_relay[t, rows, :].astype(f32)).astype(bf16)

        @pl.when(odd == 0)
        def _():
            for t in range(2):
                kv_copy(t, 0, chunk, XN, True).start()

        @pl.when(odd == 1)
        def _():
            for t in range(2):
                kv_copy(t, 1, chunk, XP, True).start()
        return 0

    lax.fori_loop(0, HEADS, sum_pair, 0)

    def sum_all(j, _):
        chunk = chunk_at(j)
        rows = local_rows(chunk)
        pair_copy(0, chunk).wait_recv()
        far_copy(chunk).wait_recv()
        mine = jnp.where(near(chunk), 0, 1)
        low_q[rows, :] = (q_near[mine, rows, :].astype(f32) + dq_pair[0, rows, :].astype(f32)
                          + dq_far[rows, :].astype(f32)).astype(bf16)
        pl.when(j < HEADS - 1)(lambda: out_copy(0, chunk).start())
        for t in range(2):
            total = kv_near[t, 2, rows, :].astype(f32)
            for x in range(2):
                kv_copy(t, x, chunk, XN).wait_recv()
                total = total + kv_far[t, x, rows, :].astype(f32)
            (low_k, low_v)[t][rows, :] = total.astype(bf16)

        @pl.when(j < HEADS - 1)
        def _():
            for t in (1, 2):
                out_copy(t, chunk).start()
        return 0

    lax.fori_loop(0, HEADS, sum_all, 0)
    own = []
    for t in range(3):
        low, out, wide = ((low_q, gq, 256), (low_k, gk, 128), (low_v, gv, 128))[t]
        own.append(pltpu.make_async_copy(low.at[local_rows(head)],
                                         out.at[:, pl.ds(pl.multiple_of(head * wide, wide), wide)], own_sem.at[t]))
        own[-1].start()

    def finish(j, _):
        chunk = chunk_at(j)
        for which in range(2):
            pair_copy(which, chunk).wait_send()
        far_copy(chunk).wait_send()
        for t in range(2):
            for x in range(3):
                kv_copy(t, x, chunk, XN).wait_send()

        @pl.when(j < HEADS - 1)
        def _():
            for t in range(3):
                low, out, wide = ((low_q, gq, 256), (low_k, gk, 128), (low_v, gv, 128))[t]
                out_copy(t, chunk).wait_send()
                remote(low.at[local_rows(head)], out.at[:, pl.ds(pl.multiple_of(chunk * wide, wide), wide)],
                       send_out.at[t, head], recv_out.at[t, chunk], {"head": chunk}).wait_recv()
        return 0

    lax.fori_loop(0, HEADS, finish, 0)
    for copy in own:
        copy.wait()


def collect(dq, dk, dv):
    hbm = pl.BlockSpec(memory_space=pl.ANY)
    wide, narrow = (CTX_ROWS, 256), (CTX_ROWS, 128)
    return pl.pallas_call(
        collect_kernel,
        out_shape=(jax.ShapeDtypeStruct((BLK, 2048), bf16), jax.ShapeDtypeStruct((BLK, 1024), bf16),
                   jax.ShapeDtypeStruct((BLK, 1024), bf16)),
        in_specs=[hbm] * 3,
        out_specs=(hbm,) * 3,
        scratch_shapes=[pltpu.VMEM((2,) + wide, bf16), pltpu.VMEM((2, 3) + narrow, bf16),
                        pltpu.VMEM((2,) + wide, bf16), pltpu.VMEM(wide, bf16), pltpu.VMEM(wide, bf16),
                        pltpu.VMEM((2, 2) + narrow, bf16), pltpu.VMEM((2,) + narrow, bf16), pltpu.VMEM((2,) + narrow, bf16),
                        pltpu.VMEM(wide, bf16), pltpu.VMEM(narrow, bf16), pltpu.VMEM(narrow, bf16),
                        pltpu.SemaphoreType.DMA((9, HEADS)), pltpu.SemaphoreType.DMA((9, HEADS)),
                        pltpu.SemaphoreType.DMA((3, HEADS)), pltpu.SemaphoreType.DMA((3, HEADS)),
                        pltpu.SemaphoreType.DMA((8,))],
        compiler_params=pltpu.CompilerParams(collective_id=2, has_side_effects=True, vmem_limit_bytes=60 * 2**20),
        name="collect",
    )(dq, dk, dv)


def hand_over_kernel(a, b, c, x, y, z):
    x[...] = a[...]
    y[...] = b[...]
    z[...] = c[...]


def hand_over(*arrays):
    vm = pl.BlockSpec(memory_space=pltpu.VMEM)
    return pl.pallas_call(
        hand_over_kernel,
        out_shape=tuple(jax.ShapeDtypeStruct(a.shape, a.dtype) for a in arrays),
        in_specs=[vm] * 3, out_specs=(vm,) * 3,
        compiler_params=pltpu.CompilerParams(vmem_limit_bytes=60 * 2**20),
        name="hand_over",
    )(*arrays)


def local(queries, keys, values, output, grad_output, positions):
    q, do, k, v, aux_r, aux_k, part = spread(queries, grad_output, keys, values, output, positions.reshape(1, BLK))
    z, tiles = totals(q, k, aux_r, aux_k, part)
    dq, dk, dv = grads(tiles, q, do, k, v, pool(z), aux_r, aux_k)
    return hand_over(*collect(dq, dk, dv))


def solution(mesh):
    rows = P(("head", "inner", "outer"), None)
    return jax.shard_map(
        local, mesh=mesh,
        in_specs=(rows,) * 5 + (P(("head", "inner", "outer")),),
        out_specs=(rows,) * 3,
        check_vma=False,
    )
```

```python
import functools, math
import jax, jax.numpy as jnp
from jax import lax
from jax.experimental import pallas as pl
from jax.experimental.pallas import tpu as pltpu
from jax.sharding import PartitionSpec as P

f32, bf16 = jnp.float32, jnp.bfloat16
HD = 128
TILE = 512
STRIP = 256
SCALE = 1.0 / 600.0
CAP2 = 50.0 * math.log2(math.e)

def nt(a, b):
    return lax.dot_general(a, b, (((1,), (1,)), ((), ())), preferred_element_type=f32)

def nn(a, b):
    return lax.dot_general(a, b, (((1,), (0,)), ((), ())), preferred_element_type=f32)

def place_of(aux, block):
    part = aux[block // 2, pl.ds(pl.multiple_of(lax.rem(block, 2) * 4, 4), 4), 2:3, :]
    return jnp.concatenate([part[c] for c in range(4)], axis=1)


def delta_of(aux, block, h):
    part = aux[block // 2, pl.ds(pl.multiple_of(lax.rem(block, 2) * 4, 4), 4), h:h + 1, :]
    return jnp.concatenate([part[c] for c in range(4)], axis=1)


def column(row):
    return jnp.broadcast_to(row, (HD, TILE)).T


def widen(col):
    return jnp.concatenate([col] * (TILE // HD), axis=1)


WHOLE, PARTLY = 0, 4096


def live_tiles(nr, nk, aux_r, aux_k, span, tiles, rest):
    for b in range(nr):
        part = aux_r[b // 2, 4 * (b % 2):4 * (b % 2) + 4, 2, :]
        span[0, b] = jnp.min(part)
        span[1, b] = jnp.max(part)
    for b in range(nk):
        part = aux_k[b // 2, 4 * (b % 2):4 * (b % 2) + 4, 2, :]
        span[2, b] = jnp.min(part)
        span[3, b] = jnp.max(part)
    tiles[1] = nr * 64 + nk

    def scan(i, counts):
        n, m = counts
        kb, rb = i // nr, lax.rem(i, nr)
        some = span[2, kb] <= span[1, rb]
        whole = span[3, kb] <= span[0, rb]

        @pl.when(some)
        def _():
            code = jnp.where(whole, WHOLE, PARTLY) + rb * 64 + kb
            tiles[n + 2] = code
            rest[m] = code
        step = some.astype(jnp.int32)
        made = jnp.logical_and(lax.rem(rb, 2) == 1, lax.rem(kb, 2) == 0)
        return n + step, m + jnp.where(made, 0, step)

    n, m = lax.fori_loop(0, nr * nk, scan, (0, 0))
    tiles[0] = n
    tiles[n + 2] = nr * 64 + nk
    return m


def totals_kernel(nr, nk, q_ref, k_ref, aux_r, aux_k, part_ref, z_ref, tiles, span, rest):
    for b in range(nr):
        z_ref[b] = part_ref[b // 2] if b % 2 else jnp.zeros((2, 8, TILE), f32)
    count = live_tiles(nr, nk, aux_r, aux_k, span, tiles, rest)

    def tile(rb, kb, masked):
        rows = pl.ds(pl.multiple_of(rb * TILE, TILE), TILE)
        kk = k_ref[pl.ds(pl.multiple_of(kb * TILE, TILE), TILE), :]
        if masked:
            live = widen(column(place_of(aux_k, kb))) <= place_of(aux_r, rb)
        for h in range(2):
            s = nt(kk, q_ref[rows, h * HD:(h + 1) * HD])
            e = jnp.exp2(jnp.tanh(s * SCALE) * CAP2)
            if masked:
                e = jnp.where(live, e, 0.0)
            z_ref[rb, h] += jnp.sum(e.reshape(TILE // 8, 8, TILE), axis=0)

    def step(i, _):
        code = rest[i]
        rb, kb = (code // 64) % 64, code % 64
        pl.when(code < PARTLY)(lambda: tile(rb, kb, False))
        pl.when(code >= PARTLY)(lambda: tile(rb, kb, True))
        return 0

    lax.fori_loop(0, count, step, 0)


def totals(q, k, aux_r, aux_k, part):
    nr, nk = q.shape[0] // TILE, k.shape[0] // TILE
    vm = pl.BlockSpec(memory_space=pltpu.VMEM)
    return pl.pallas_call(
        functools.partial(totals_kernel, nr, nk),
        out_shape=(jax.ShapeDtypeStruct((nr, 2, 8, TILE), f32), jax.ShapeDtypeStruct((nr * nk + 8,), jnp.int32)),
        in_specs=[vm] * 5,
        out_specs=(vm, pl.BlockSpec(memory_space=pltpu.SMEM)),
        scratch_shapes=[pltpu.SMEM((4, 8), f32), pltpu.SMEM((nr * nk + 8,), jnp.int32)],
        compiler_params=pltpu.CompilerParams(vmem_limit_bytes=60 * 2**20),
        cost_estimate=pl.CostEstimate(flops=2 * 10**10, bytes_accessed=4 * 2**20, transcendentals=3 * 10**7),
        name="totals",
    )(q, k, aux_r, aux_k, part)


def grads_kernel(nr, nk, tiles, q_ref, do_ref, k_ref, v_ref, z_ref, aux_r, aux_k,
                 dq_ref, dk_ref, dv_ref, qt, dot, dq, dkt, dvt, lcol, dcol, wbuf, gbuf):
    dq[...] = jnp.zeros_like(dq)
    dkt[...] = jnp.zeros_like(dkt)
    dvt[...] = jnp.zeros_like(dvt)

    def prep(rb, _):
        rows = pl.ds(pl.multiple_of(rb * TILE, TILE), TILE)
        for h in range(2):
            cols = slice(h * HD, (h + 1) * HD)
            hr = slice(h * TILE, (h + 1) * TILE)
            qt[rb, :, hr] = q_ref[rows, cols].T
            dot[rb, :, hr] = do_ref[rows, cols].T
            lcol[rb, hr, :] = column(jnp.log2(z_ref[rb, h:h + 1, :]))
            dcol[rb, hr, :] = column(delta_of(aux_r, rb, h))
        return 0

    lax.fori_loop(0, nr, prep, 0)

    def keys_of(ref, kb):
        return ref[pl.ds(pl.multiple_of(kb * TILE, TILE), TILE), :]

    def body(i, masked):
        now, last = tiles[i + 2], tiles[i + 1]
        rc, kc = (last // 64) % 64, last % 64
        ra, ka = jnp.minimum((now // 64) % 64, nr - 1), jnp.minimum(now % 64, nk - 1)
        kk = keys_of(k_ref, ka)
        vv = keys_of(v_ref, ka)
        kcc = keys_of(k_ref, jnp.minimum(kc, nk - 1))
        if masked:
            live = place_of(aux_k, ka) <= widen(column(place_of(aux_r, ra)))
        dv_sum, dk_sum = dvt[kc], dkt[kc]
        for c in range(2 * TILE // STRIP):
            hr = slice(c * STRIP, (c + 1) * STRIP)
            w, g = wbuf[hr, :], gbuf[hr, :]
            dv_sum = dv_sum + nn(dot[rc, :, hr], w)
            dk_sum = dk_sum + nn(qt[rc, :, hr], g)
            dq[rc, hr, :] += nn(g, kcc)
            rows = pl.ds(pl.multiple_of(ra * TILE + c * STRIP % TILE, STRIP), STRIP)
            cols = slice(c * STRIP // TILE * HD, (c * STRIP // TILE + 1) * HD)
            t = jnp.tanh(nt(q_ref[rows, cols], kk) * SCALE)
            p = nt(do_ref[rows, cols], vv)
            w = jnp.exp2(t * CAP2 - widen(lcol[ra, hr, :]))
            if masked:
                lo = c * STRIP % TILE
                w = jnp.where(live[lo:lo + STRIP], w, 0.0)
            g = w * (p - widen(dcol[ra, hr, :])) * (1.0 - t * t)
            wbuf[hr, :] = w.astype(bf16)
            gbuf[hr, :] = g.astype(bf16)
        dvt[kc] = dv_sum
        dkt[kc] = dk_sum

    def step(i, _):
        masked = tiles[i + 2] >= PARTLY
        pl.when(jnp.logical_not(masked))(lambda: body(i, False))
        pl.when(masked)(lambda: body(i, True))
        return 0

    lax.fori_loop(0, tiles[0] + 1, step, 0)

    def out_rows(rb, _):
        rows = pl.ds(pl.multiple_of(rb * TILE, TILE), TILE)
        for h in range(2):
            dq_ref[rows, h * HD:(h + 1) * HD] = (dq[rb, h * TILE:(h + 1) * TILE, :] * (1.0 / 12.0)).astype(bf16)
        return 0

    def out_keys(kb, _):
        keys = pl.ds(pl.multiple_of(kb * TILE, TILE), TILE)
        dk_ref[keys, :] = (dkt[kb] * (1.0 / 12.0)).T.astype(bf16)
        dv_ref[keys, :] = dvt[kb].T.astype(bf16)
        return 0

    lax.fori_loop(0, nr, out_rows, 0)
    lax.fori_loop(0, nk, out_keys, 0)


def grads(tiles, q, do, k, v, z, aux_r, aux_k):
    nr, nk = q.shape[0] // TILE, k.shape[0] // TILE
    vm = pl.BlockSpec(memory_space=pltpu.VMEM)
    return pl.pallas_call(
        functools.partial(grads_kernel, nr, nk),
        out_shape=(jax.ShapeDtypeStruct(q.shape, bf16), jax.ShapeDtypeStruct(k.shape, bf16), jax.ShapeDtypeStruct(k.shape, bf16)),
        in_specs=[pl.BlockSpec(memory_space=pltpu.SMEM)] + [vm] * 7,
        out_specs=(vm,) * 3,
        scratch_shapes=[
            pltpu.VMEM((nr + 1, HD, 2 * TILE), bf16), pltpu.VMEM((nr + 1, HD, 2 * TILE), bf16),
            pltpu.VMEM((nr + 1, 2 * TILE, HD), f32),
            pltpu.VMEM((nk + 1, HD, TILE), f32), pltpu.VMEM((nk + 1, HD, TILE), f32),
            pltpu.VMEM((nr, 2 * TILE, HD), f32), pltpu.VMEM((nr, 2 * TILE, HD), f32),
            pltpu.VMEM((2 * TILE, TILE), bf16), pltpu.VMEM((2 * TILE, TILE), bf16),
        ],
        compiler_params=pltpu.CompilerParams(vmem_limit_bytes=60 * 2**20),
        cost_estimate=pl.CostEstimate(flops=5 * 10**10, bytes_accessed=16 * 2**20, transcendentals=3 * 10**7),
        name="grads",
    )(tiles, q, do, k, v, z, aux_r, aux_k)


MESH = pl.DeviceIdType.MESH
HEADS, INNER, OUTER, BLK, CTX_ROWS = 8, 4, 4, 128, 1024


def peers():
    head, inner, outer = (lax.axis_index(a) for a in ("head", "inner", "outer"))
    y_peer = lax.rem(inner + 2, INNER)
    core_peer = inner + 1 - 2 * lax.rem(inner, 2)
    x_next, x_prev = lax.rem(outer + 1, OUTER), lax.rem(outer + OUTER - 1, OUTER)
    return head, inner, outer, y_peer, core_peer, x_next, x_prev


def neighbours():
    head, inner, outer, y_peer, core_peer, x_next, x_prev = peers()
    across = (1 - head // 4) * 4
    return ([{"head": lax.rem(head + j, HEADS)} for j in range(1, HEADS)]
            + [{"head": across + z, "inner": y_peer} for z in range(4)]
            + [{"inner": y_peer}, {"inner": core_peer}, {"outer": x_next}, {"outer": x_prev}])


def greet(devices):
    barrier = pltpu.get_barrier_semaphore()
    for device in devices:
        pl.semaphore_signal(barrier, inc=1, device_id=device, device_id_type=MESH)
    pl.semaphore_wait(barrier, len(devices))


def rows_at(ref, block, chunk):
    return ref.at[pl.ds(pl.multiple_of(block * CTX_ROWS + chunk * BLK, BLK), BLK)]


def spread_kernel(q, do, k, v, out, pos, q_all, do_all, k_all, v_all, aux_r, aux_k, z_ref,
                  aux, send1, recv1, send2, recv2, own_sem):
    head, inner, outer, y_peer, core_peer, x_next, x_prev = peers()
    greet(neighbours())

    def aux_at(ref, block, chunk):
        return ref.at[block, chunk]

    def fill_aux():
        for g in range(HEADS):
            aux[g, 2:8, :] = jnp.broadcast_to(pos[...].astype(f32), (6, BLK))
            for h in range(2):
                cols = slice((2 * g + h) * HD, (2 * g + h + 1) * HD)
                product = do[:, cols].astype(f32) * out[:, cols].astype(f32)
                aux[g, h:h + 1, :] = jnp.sum(product.T, axis=0, keepdims=True)

    def near(chunk):
        return chunk // 4 == head // 4

    def via(t, dest):
        if t in (0, 1, 4):
            return {"head": dest, "inner": jnp.where(near(dest), inner, y_peer)}
        return {"head": dest}

    def first(t, dest, source_head):
        if t == 4:
            return aux.at[dest], aux_at(aux_r, inner, source_head)
        if t == 5:
            return aux.at[dest], aux_at(aux_k, outer, source_head)
        src = (q, do, k, v)[t]
        dst = (q_all, do_all, k_all, v_all)[t]
        wide = 256 if t < 2 else 128
        return (src.at[:, pl.ds(pl.multiple_of(dest * wide, wide), wide)],
                rows_at(dst, inner if t < 2 else outer, source_head))

    def remote(src, dst, ssem, rsem, device):
        return pltpu.make_async_remote_copy(src_ref=src, dst_ref=dst, send_sem=ssem, recv_sem=rsem,
                                            device_id=device, device_id_type=MESH)

    ORDER = (0, 2, 4, 5, 3, 1)
    def send_part(part):
        for t in part:
            src, dst = first(t, head, head)
            pltpu.make_async_copy(src, dst, own_sem.at[t]).start()

        def send_first(j, _):
            dest = lax.rem(head + j, HEADS)
            for t in part:
                src, dst = first(t, dest, head)
                remote(src, dst, send1.at[t, dest], recv1.at[t, head], via(t, dest)).start()
            return 0

        lax.fori_loop(1, HEADS, send_first, 0)

    EARLY, LATE = (0, 2, 4, 5), (1, 3)
    send_part((0, 2))
    fill_aux()
    send_part((4, 5))
    send_part(LATE)

    def wait_own(part):
        for t in part:
            src, dst = first(t, head, head)
            pltpu.make_async_copy(src, dst, own_sem.at[t]).wait()

    wait_own(EARLY)

    y_core = lax.rem(core_peer + 2, INNER)
    x_far = lax.rem(outer + 2, OUTER)

    def base(g):
        return 4 * (head // 4) if g == 0 else 4 * (1 - head // 4)

    def piece(t, block, g):
        if t >= 4:
            return (aux_r, aux_k)[t - 4].at[block, pl.ds(base(g), 4)]
        return (q_all, do_all, k_all, v_all)[t].at[pl.ds(pl.multiple_of(block * CTX_ROWS + base(g) * BLK, 4 * BLK), 4 * BLK)]

    ROWS, KEYS = (0, 4, 1), (2, 5, 3)

    def hop(route, t, block, g, device):
        ref = piece(t, block, g)
        s = (ROWS if t in ROWS else KEYS).index(t)
        return remote(ref, ref, send2.at[route, s, g], recv2.at[route, s, g], device)

    Y, C, XN, XP = {"inner": y_peer}, {"inner": core_peer}, {"outer": x_next}, {"outer": x_prev}

    def forward(part, g):
        def wait_first(chunk):
            for t in part:
                src, dst = first(t, head, chunk)
                remote(src, dst, send1.at[t, chunk], recv1.at[t, chunk], {"head": chunk}).wait_recv()

        for n in range(4):
            chunk = base(g) + lax.rem(head + 4 - n, 4)
            if g == 1 or n > 0:
                wait_first(chunk)
        for t in part:
            if t in ROWS:
                block = inner if g == 0 else y_peer
                hop(0, t, block, g, Y).start()
                hop(1, t, block, g, C).start()
            else:
                hop(3, t, outer, g, XN).start()
                hop(4, t, outer, g, XP).start()

    def relay(part, g):
        for t in part:
            if t in ROWS:
                block = y_peer if g == 0 else inner
                hop(0, t, block, g, Y).wait_recv()
                hop(2, t, block, g, C).start()
        for t in part:
            if t in KEYS:
                hop(3, t, x_prev, g, XN).wait_recv()
                hop(4, t, x_next, g, XP).wait_recv()
                if g == 0:
                    hop(5, t, x_prev, g, XN).start()
                else:
                    hop(5, t, x_next, g, XP).start()

    def arrive(part):
        for g in range(2):
            for t in part:
                if t in ROWS:
                    hop(1, t, core_peer, g, C).wait_recv()
                    hop(2, t, y_core, g, C).wait_recv()
                else:
                    hop(5, t, x_far, g, XN).wait_recv()

    def tile(n):
        r, c = n // 4, lax.rem(n, 4)
        live = widen(column(place_of(aux_k, 2 * c))) <= place_of(aux_r, 2 * r + 1)
        kk = k_all[pl.ds(pl.multiple_of(c * CTX_ROWS, CTX_ROWS), TILE), :]
        rows = pl.ds(pl.multiple_of(r * CTX_ROWS + TILE, TILE), TILE)
        for h in range(2):
            e = jnp.exp2(jnp.tanh(nt(kk, q_all[rows, h * HD:(h + 1) * HD]) * SCALE) * CAP2)
            z_ref[r, h] += jnp.sum(jnp.where(live, e, 0.0).reshape(TILE // 8, 8, TILE), axis=0)

    def some_tiles(start, stop):
        def step(n, _):
            tile(n)
            return 0
        lax.fori_loop(start, stop, step, 0)

    forward(EARLY, 0)
    forward(EARLY, 1)
    z_ref[...] = jnp.zeros_like(z_ref)
    wait_own(LATE)
    relay(EARLY, 0)
    forward(LATE, 0)
    relay(EARLY, 1)
    forward(LATE, 1)
    arrive(EARLY)
    some_tiles(0, 4)
    relay(LATE, 0)
    some_tiles(4, 10)
    relay(LATE, 1)
    some_tiles(10, 16)
    arrive(LATE)

    for g in range(2):
        for t in ROWS:
            hop(0, t, inner, g, Y).wait_send()
            hop(1, t, inner, g, C).wait_send()
            hop(2, t, y_peer, g, C).wait_send()
        for t in KEYS:
            hop(3, t, outer, g, XN).wait_send()
            hop(4, t, outer, g, XP).wait_send()
            hop(5, t, x_prev, g, XN).wait_send()

    def finish(j, _):
        chunk = lax.rem(head + HEADS - j, HEADS)
        for t in ORDER:
            src, dst = first(t, chunk, head)
            remote(src, dst, send1.at[t, chunk], recv1.at[t, chunk], {"head": chunk}).wait_send()
        return 0

    lax.fori_loop(1, HEADS, finish, 0)


def spread(q, do, k, v, out, pos):
    hbm = pl.BlockSpec(memory_space=pl.ANY)
    vm = pl.BlockSpec(memory_space=pltpu.VMEM)
    rows = INNER * CTX_ROWS
    return pl.pallas_call(
        spread_kernel,
        out_shape=(jax.ShapeDtypeStruct((rows, 256), bf16), jax.ShapeDtypeStruct((rows, 256), bf16),
                   jax.ShapeDtypeStruct((rows, 128), bf16), jax.ShapeDtypeStruct((rows, 128), bf16),
                   jax.ShapeDtypeStruct((INNER, HEADS, 8, 128), f32), jax.ShapeDtypeStruct((OUTER, HEADS, 8, 128), f32),
                   jax.ShapeDtypeStruct((INNER, 2, 8, TILE), f32)),
        in_specs=[vm] * 6,
        out_specs=(vm, hbm, vm, hbm, vm, vm, vm),
        scratch_shapes=[pltpu.VMEM((HEADS, 8, 128), f32),
                        pltpu.SemaphoreType.DMA((6, HEADS)), pltpu.SemaphoreType.DMA((6, HEADS)),
                        pltpu.SemaphoreType.DMA((6, 3, 2)), pltpu.SemaphoreType.DMA((6, 3, 2)),
                        pltpu.SemaphoreType.DMA((6,))],
        compiler_params=pltpu.CompilerParams(collective_id=0, has_side_effects=True, vmem_limit_bytes=60 * 2**20),
        name="spread",
    )(q, do, k, v, out, pos)


def pool_kernel(z, out, recv, send_sem, recv_sem):
    head, inner, outer, y_peer, core_peer, x_next, x_prev = peers()
    others = [lax.rem(inner + j, INNER) for j in range(1, INNER)]
    greet([{"inner": o} for o in others])
    out[...] = jnp.sum(z[...], axis=2)
    copies = []
    for j, o in enumerate(others):
        copies.append(pltpu.make_async_remote_copy(
            src_ref=out, dst_ref=recv.at[j], send_sem=send_sem.at[j], recv_sem=recv_sem.at[j],
            device_id={"inner": o}, device_id_type=MESH))
        copies[-1].start()
    for c in copies:
        c.wait()
    total = jnp.zeros(out.shape, f32)
    for i in range(INNER):
        d = lax.rem(inner - i + INNER, INNER)
        part = jnp.where(d == 0, out[...], jnp.where(d == 1, recv[0], jnp.where(d == 2, recv[1], recv[2])))
        total = total + part
    out[...] = total


def pool(z):
    vm = pl.BlockSpec(memory_space=pltpu.VMEM)
    small = (z.shape[0], 2, z.shape[3])
    return pl.pallas_call(
        pool_kernel,
        out_shape=jax.ShapeDtypeStruct(small, f32),
        in_specs=[vm], out_specs=vm,
        scratch_shapes=[pltpu.VMEM((3,) + small, f32), pltpu.SemaphoreType.DMA((3,)), pltpu.SemaphoreType.DMA((3,))],
        compiler_params=pltpu.CompilerParams(collective_id=1, has_side_effects=True),
        name="pool",
    )(z)


def collect_kernel(dq, dk, dv, gq, gk, gv, q_near, kv_near, dq_pair, dq_sum, dq_far, kv_far, kv_relay, kv_sum,
                   low_q, low_k, low_v, send_sem, recv_sem, send_out, recv_out, own_sem):
    head, inner, outer, y_peer, core_peer, x_next, x_prev = peers()
    x_far = lax.rem(outer + 2, OUTER)

    def block_rows(block):
        return pl.ds(pl.multiple_of(block * CTX_ROWS, CTX_ROWS), CTX_ROWS)

    held = [pltpu.make_async_copy(dq.at[block_rows(y_peer)], q_near.at[1], own_sem.at[0]),
            pltpu.make_async_copy(dq.at[block_rows(inner)], q_near.at[0], own_sem.at[1])]
    for t in range(2):
        for x, block in enumerate((x_next, x_prev, outer)):
            held.append(pltpu.make_async_copy((dk, dv)[t].at[block_rows(block)], kv_near.at[t, x], own_sem.at[2 + 3 * t + x]))
    for copy in held:
        copy.start()
    greet(neighbours())
    y_core = lax.rem(core_peer + 2, INNER)
    Y, C, XN, XP = {"inner": y_peer}, {"inner": core_peer}, {"outer": x_next}, {"outer": x_prev}

    def remote(src, dst, ssem, rsem, device):
        return pltpu.make_async_remote_copy(src_ref=src, dst_ref=dst, send_sem=ssem, recv_sem=rsem,
                                            device_id=device, device_id_type=MESH)

    def local_rows(chunk):
        return pl.ds(pl.multiple_of(chunk * BLK, BLK), BLK)

    def near(chunk):
        return chunk // 4 == head // 4

    def pair_copy(which, chunk):
        block = jnp.where(near(chunk), *((core_peer, y_core) if which == 0 else (y_core, core_peer)))
        return remote(rows_at(dq, block, chunk), dq_pair.at[which, local_rows(chunk)],
                      send_sem.at[which, chunk], recv_sem.at[which, chunk], C)

    def far_copy(chunk):
        return remote(dq_sum.at[local_rows(chunk)], dq_far.at[local_rows(chunk)],
                      send_sem.at[2, chunk], recv_sem.at[2, chunk], Y)

    def kv_copy(t, x, chunk, device, summed=False):
        n = 3 + 3 * t + x
        src = kv_sum.at[t, local_rows(chunk)] if summed else rows_at((dk, dv)[t], (x_next, x_prev, x_far)[x], chunk)
        dst = kv_relay.at[t, local_rows(chunk)] if x == 2 else kv_far.at[t, x, local_rows(chunk)]
        return remote(src, dst, send_sem.at[n, chunk], recv_sem.at[n, chunk], device)

    def out_copy(t, chunk):
        low, out, wide = ((low_q, gq, 256), (low_k, gk, 128), (low_v, gv, 128))[t]
        device = {"head": chunk, "inner": jnp.where(near(chunk), inner, y_peer)} if t == 0 else {"head": chunk}
        return remote(low.at[local_rows(chunk)], out.at[:, pl.ds(pl.multiple_of(head * wide, wide), wide)],
                      send_out.at[t, chunk], recv_out.at[t, head], device)

    def chunk_at(j):
        return lax.rem(head + 1 + j, HEADS)

    def each_chunk(fn):
        def step(j, _):
            fn(j, chunk_at(j))
            return 0
        lax.fori_loop(0, HEADS, step, 0)

    def by_parity(chunk, even, odd):
        pl.when(lax.rem(chunk, 2) == 0)(lambda: [even(t) for t in range(2)] and None)
        pl.when(lax.rem(chunk, 2) == 1)(lambda: [odd(t) for t in range(2)] and None)

    def send_through(j, chunk):
        pair_copy(1, chunk).start()
        by_parity(chunk, lambda t: kv_copy(t, 2, chunk, XN).start(), lambda t: kv_copy(t, 2, chunk, XP).start())

    def send_direct(j, chunk):
        pair_copy(0, chunk).start()
        by_parity(chunk, lambda t: kv_copy(t, 1, chunk, XP).start(), lambda t: kv_copy(t, 0, chunk, XN).start())

    each_chunk(send_through)
    each_chunk(send_direct)
    for copy in held:
        copy.wait()

    def sum_pair(j, chunk):
        rows = local_rows(chunk)
        pair_copy(1, chunk).wait_recv()
        mine = jnp.where(near(chunk), 0, 1)
        dq_sum[rows, :] = (q_near[1 - mine, rows, :].astype(f32) + dq_pair[1, rows, :].astype(f32)).astype(bf16)
        far_copy(chunk).start()

    def sum_relay(j, chunk):
        rows = local_rows(chunk)
        odd = lax.rem(chunk, 2)
        for t in range(2):
            kv_copy(t, 2, chunk, XN).wait_recv()
            kv_sum[t, rows, :] = (kv_near[t, odd, rows, :].astype(f32) + kv_relay[t, rows, :].astype(f32)).astype(bf16)
        by_parity(chunk, lambda t: kv_copy(t, 0, chunk, XN, True).start(), lambda t: kv_copy(t, 1, chunk, XP, True).start())

    each_chunk(sum_pair)
    each_chunk(sum_relay)

    def finish_rows(j, chunk):
        rows = local_rows(chunk)
        pair_copy(0, chunk).wait_recv()
        far_copy(chunk).wait_recv()
        mine = jnp.where(near(chunk), 0, 1)
        low_q[rows, :] = (q_near[mine, rows, :].astype(f32) + dq_pair[0, rows, :].astype(f32)
                          + dq_far[rows, :].astype(f32)).astype(bf16)
        pl.when(j < HEADS - 1)(lambda: out_copy(0, chunk).start())

    def finish_keys(j, chunk):
        rows = local_rows(chunk)
        for t in range(2):
            total = kv_near[t, 2, rows, :].astype(f32)
            for x in range(2):
                kv_copy(t, x, chunk, XN).wait_recv()
                total = total + kv_far[t, x, rows, :].astype(f32)
            (low_k, low_v)[t][rows, :] = total.astype(bf16)

        @pl.when(j < HEADS - 1)
        def _():
            for t in (1, 2):
                out_copy(t, chunk).start()

    def finish_both(j, chunk):
        finish_rows(j, chunk)
        finish_keys(j, chunk)

    each_chunk(finish_both)
    own = []
    for t in range(3):
        low, out, wide = ((low_q, gq, 256), (low_k, gk, 128), (low_v, gv, 128))[t]
        own.append(pltpu.make_async_copy(low.at[local_rows(head)],
                                         out.at[:, pl.ds(pl.multiple_of(head * wide, wide), wide)], own_sem.at[t]))
        own[-1].start()

    def finish(j, _):
        chunk = chunk_at(j)
        for which in range(2):
            pair_copy(which, chunk).wait_send()
        far_copy(chunk).wait_send()
        for t in range(2):
            for x in range(3):
                kv_copy(t, x, chunk, XN).wait_send()

        @pl.when(j < HEADS - 1)
        def _():
            for t in range(3):
                low, out, wide = ((low_q, gq, 256), (low_k, gk, 128), (low_v, gv, 128))[t]
                out_copy(t, chunk).wait_send()
                remote(low.at[local_rows(head)], out.at[:, pl.ds(pl.multiple_of(chunk * wide, wide), wide)],
                       send_out.at[t, head], recv_out.at[t, chunk], {"head": chunk}).wait_recv()
        return 0

    lax.fori_loop(0, HEADS, finish, 0)
    for copy in own:
        copy.wait()


def collect(dq, dk, dv):
    hbm = pl.BlockSpec(memory_space=pl.ANY)
    wide, narrow = (CTX_ROWS, 256), (CTX_ROWS, 128)
    return pl.pallas_call(
        collect_kernel,
        out_shape=(jax.ShapeDtypeStruct((BLK, 2048), bf16), jax.ShapeDtypeStruct((BLK, 1024), bf16),
                   jax.ShapeDtypeStruct((BLK, 1024), bf16)),
        in_specs=[hbm] * 3,
        out_specs=(hbm,) * 3,
        scratch_shapes=[pltpu.VMEM((2,) + wide, bf16), pltpu.VMEM((2, 3) + narrow, bf16),
                        pltpu.VMEM((2,) + wide, bf16), pltpu.VMEM(wide, bf16), pltpu.VMEM(wide, bf16),
                        pltpu.VMEM((2, 2) + narrow, bf16), pltpu.VMEM((2,) + narrow, bf16), pltpu.VMEM((2,) + narrow, bf16),
                        pltpu.VMEM(wide, bf16), pltpu.VMEM(narrow, bf16), pltpu.VMEM(narrow, bf16),
                        pltpu.SemaphoreType.DMA((9, HEADS)), pltpu.SemaphoreType.DMA((9, HEADS)),
                        pltpu.SemaphoreType.DMA((3, HEADS)), pltpu.SemaphoreType.DMA((3, HEADS)),
                        pltpu.SemaphoreType.DMA((8,))],
        compiler_params=pltpu.CompilerParams(collective_id=2, has_side_effects=True, vmem_limit_bytes=60 * 2**20),
        name="collect",
    )(dq, dk, dv)


def hand_over_kernel(a, b, c, x, y, z):
    x[...] = a[...]
    y[...] = b[...]
    z[...] = c[...]


def hand_over(*arrays):
    vm = pl.BlockSpec(memory_space=pltpu.VMEM)
    return pl.pallas_call(
        hand_over_kernel,
        out_shape=tuple(jax.ShapeDtypeStruct(a.shape, a.dtype) for a in arrays),
        in_specs=[vm] * 3, out_specs=(vm,) * 3,
        compiler_params=pltpu.CompilerParams(vmem_limit_bytes=60 * 2**20),
        name="hand_over",
    )(*arrays)


def local(queries, keys, values, output, grad_output, positions):
    q, do, k, v, aux_r, aux_k, part = spread(queries, grad_output, keys, values, output, positions.reshape(1, BLK))
    z, tiles = totals(q, k, aux_r, aux_k, part)
    dq, dk, dv = grads(tiles, q, do, k, v, pool(z), aux_r, aux_k)
    return hand_over(*collect(dq, dk, dv))


def solution(mesh):
    rows = P(("head", "inner", "outer"), None)
    return jax.shard_map(
        local, mesh=mesh,
        in_specs=(rows,) * 5 + (P(("head", "inner", "outer")),),
        out_specs=(rows,) * 3,
        check_vma=False,
    )
```

```python
import functools, math
import jax, jax.numpy as jnp
from jax import lax
from jax.experimental import pallas as pl
from jax.experimental.pallas import tpu as pltpu
from jax.sharding import PartitionSpec as P

f32, bf16 = jnp.float32, jnp.bfloat16
HD = 128
TILE = 512
STRIP = 256
SCALE = 1.0 / 600.0
CAP2 = 50.0 * math.log2(math.e)

def nt(a, b):
    return lax.dot_general(a, b, (((1,), (1,)), ((), ())), preferred_element_type=f32)

def nn(a, b):
    return lax.dot_general(a, b, (((1,), (0,)), ((), ())), preferred_element_type=f32)

def place_of(aux, block):
    part = aux[block // 2, pl.ds(pl.multiple_of(lax.rem(block, 2) * 4, 4), 4), 2:3, :]
    return jnp.concatenate([part[c] for c in range(4)], axis=1)


def delta_of(aux, block, h):
    part = aux[block // 2, pl.ds(pl.multiple_of(lax.rem(block, 2) * 4, 4), 4), h:h + 1, :]
    return jnp.concatenate([part[c] for c in range(4)], axis=1)


def column(row):
    return jnp.broadcast_to(row, (HD, TILE)).T


def widen(col):
    return jnp.concatenate([col] * (TILE // HD), axis=1)


WHOLE, PARTLY = 0, 4096


def live_tiles(nr, nk, aux_r, aux_k, span, tiles, rest):
    for b in range(nr):
        part = aux_r[b // 2, 4 * (b % 2):4 * (b % 2) + 4, 2, :]
        span[0, b] = jnp.min(part)
        span[1, b] = jnp.max(part)
    for b in range(nk):
        part = aux_k[b // 2, 4 * (b % 2):4 * (b % 2) + 4, 2, :]
        span[2, b] = jnp.min(part)
        span[3, b] = jnp.max(part)
    tiles[1] = nr * 64 + nk

    def scan(i, counts):
        n, m = counts
        kb, rb = i // nr, lax.rem(i, nr)
        some = span[2, kb] <= span[1, rb]
        whole = span[3, kb] <= span[0, rb]

        @pl.when(some)
        def _():
            code = jnp.where(whole, WHOLE, PARTLY) + rb * 64 + kb
            tiles[n + 2] = code
            rest[m] = code
        step = some.astype(jnp.int32)
        made = jnp.logical_and(lax.rem(rb, 2) == 1, lax.rem(kb, 2) == 0)
        return n + step, m + jnp.where(made, 0, step)

    n, m = lax.fori_loop(0, nr * nk, scan, (0, 0))
    tiles[0] = n
    tiles[n + 2] = nr * 64 + nk
    return m


def totals_kernel(nr, nk, q_ref, k_ref, aux_r, aux_k, part_ref, z_ref, tiles, span, rest):
    for b in range(nr):
        z_ref[b] = part_ref[b // 2] if b % 2 else jnp.zeros((2, 8, TILE), f32)
    count = live_tiles(nr, nk, aux_r, aux_k, span, tiles, rest)

    def tile(rb, kb, masked):
        rows = pl.ds(pl.multiple_of(rb * TILE, TILE), TILE)
        kk = k_ref[pl.ds(pl.multiple_of(kb * TILE, TILE), TILE), :]
        if masked:
            live = widen(column(place_of(aux_k, kb))) <= place_of(aux_r, rb)
        for h in range(2):
            s = nt(kk, q_ref[rows, h * HD:(h + 1) * HD])
            e = jnp.exp2(jnp.tanh(s * SCALE) * CAP2)
            if masked:
                e = jnp.where(live, e, 0.0)
            z_ref[rb, h] += jnp.sum(e.reshape(TILE // 8, 8, TILE), axis=0)

    def step(i, _):
        code = rest[i]
        rb, kb = (code // 64) % 64, code % 64
        pl.when(code < PARTLY)(lambda: tile(rb, kb, False))
        pl.when(code >= PARTLY)(lambda: tile(rb, kb, True))
        return 0

    lax.fori_loop(0, count, step, 0)


def totals(q, k, aux_r, aux_k, part):
    nr, nk = q.shape[0] // TILE, k.shape[0] // TILE
    vm = pl.BlockSpec(memory_space=pltpu.VMEM)
    return pl.pallas_call(
        functools.partial(totals_kernel, nr, nk),
        out_shape=(jax.ShapeDtypeStruct((nr, 2, 8, TILE), f32), jax.ShapeDtypeStruct((nr * nk + 8,), jnp.int32)),
        in_specs=[vm] * 5,
        out_specs=(vm, pl.BlockSpec(memory_space=pltpu.SMEM)),
        scratch_shapes=[pltpu.SMEM((4, 8), f32), pltpu.SMEM((nr * nk + 8,), jnp.int32)],
        compiler_params=pltpu.CompilerParams(vmem_limit_bytes=60 * 2**20),
        cost_estimate=pl.CostEstimate(flops=2 * 10**10, bytes_accessed=4 * 2**20, transcendentals=3 * 10**7),
        name="totals",
    )(q, k, aux_r, aux_k, part)


def grads_kernel(nr, nk, tiles, q_ref, do_ref, k_ref, v_ref, z_ref, aux_r, aux_k,
                 dq_ref, dk_ref, dv_ref, qt, dot, dq, dkt, dvt, lcol, dcol, wbuf, gbuf):
    dq[...] = jnp.zeros_like(dq)
    dkt[...] = jnp.zeros_like(dkt)
    dvt[...] = jnp.zeros_like(dvt)

    def prep(rb, _):
        rows = pl.ds(pl.multiple_of(rb * TILE, TILE), TILE)
        for h in range(2):
            cols = slice(h * HD, (h + 1) * HD)
            hr = slice(h * TILE, (h + 1) * TILE)
            qt[rb, :, hr] = q_ref[rows, cols].T
            dot[rb, :, hr] = do_ref[rows, cols].T
            lcol[rb, hr, :] = column(jnp.log2(z_ref[rb, h:h + 1, :]))
            dcol[rb, hr, :] = column(delta_of(aux_r, rb, h))
        return 0

    lax.fori_loop(0, nr, prep, 0)

    def keys_of(ref, kb):
        return ref[pl.ds(pl.multiple_of(kb * TILE, TILE), TILE), :]

    def body(i, masked):
        now, last = tiles[i + 2], tiles[i + 1]
        rc, kc = (last // 64) % 64, last % 64
        ra, ka = jnp.minimum((now // 64) % 64, nr - 1), jnp.minimum(now % 64, nk - 1)
        kk = keys_of(k_ref, ka)
        vv = keys_of(v_ref, ka)
        kcc = keys_of(k_ref, jnp.minimum(kc, nk - 1))
        if masked:
            live = place_of(aux_k, ka) <= widen(column(place_of(aux_r, ra)))
        dv_sum, dk_sum = dvt[kc], dkt[kc]
        for c in range(2 * TILE // STRIP):
            hr = slice(c * STRIP, (c + 1) * STRIP)
            w, g = wbuf[hr, :], gbuf[hr, :]
            dv_sum = dv_sum + nn(dot[rc, :, hr], w)
            dk_sum = dk_sum + nn(qt[rc, :, hr], g)
            dq[rc, hr, :] += nn(g, kcc)
            rows = pl.ds(pl.multiple_of(ra * TILE + c * STRIP % TILE, STRIP), STRIP)
            cols = slice(c * STRIP // TILE * HD, (c * STRIP // TILE + 1) * HD)
            t = jnp.tanh(nt(q_ref[rows, cols], kk) * SCALE)
            p = nt(do_ref[rows, cols], vv)
            w = jnp.exp2(t * CAP2 - widen(lcol[ra, hr, :]))
            if masked:
                lo = c * STRIP % TILE
                w = jnp.where(live[lo:lo + STRIP], w, 0.0)
            g = w * (p - widen(dcol[ra, hr, :])) * (1.0 - t * t)
            wbuf[hr, :] = w.astype(bf16)
            gbuf[hr, :] = g.astype(bf16)
        dvt[kc] = dv_sum
        dkt[kc] = dk_sum

    def step(i, _):
        masked = tiles[i + 2] >= PARTLY
        pl.when(jnp.logical_not(masked))(lambda: body(i, False))
        pl.when(masked)(lambda: body(i, True))
        return 0

    lax.fori_loop(0, tiles[0] + 1, step, 0)

    def out_rows(rb, _):
        rows = pl.ds(pl.multiple_of(rb * TILE, TILE), TILE)
        for h in range(2):
            dq_ref[rows, h * HD:(h + 1) * HD] = (dq[rb, h * TILE:(h + 1) * TILE, :] * (1.0 / 12.0)).astype(bf16)
        return 0

    def out_keys(kb, _):
        keys = pl.ds(pl.multiple_of(kb * TILE, TILE), TILE)
        dk_ref[keys, :] = (dkt[kb] * (1.0 / 12.0)).T.astype(bf16)
        dv_ref[keys, :] = dvt[kb].T.astype(bf16)
        return 0

    lax.fori_loop(0, nr, out_rows, 0)
    lax.fori_loop(0, nk, out_keys, 0)


def grads(tiles, q, do, k, v, z, aux_r, aux_k):
    nr, nk = q.shape[0] // TILE, k.shape[0] // TILE
    vm = pl.BlockSpec(memory_space=pltpu.VMEM)
    return pl.pallas_call(
        functools.partial(grads_kernel, nr, nk),
        out_shape=(jax.ShapeDtypeStruct(q.shape, bf16), jax.ShapeDtypeStruct(k.shape, bf16), jax.ShapeDtypeStruct(k.shape, bf16)),
        in_specs=[pl.BlockSpec(memory_space=pltpu.SMEM)] + [vm] * 7,
        out_specs=(vm,) * 3,
        scratch_shapes=[
            pltpu.VMEM((nr + 1, HD, 2 * TILE), bf16), pltpu.VMEM((nr + 1, HD, 2 * TILE), bf16),
            pltpu.VMEM((nr + 1, 2 * TILE, HD), f32),
            pltpu.VMEM((nk + 1, HD, TILE), f32), pltpu.VMEM((nk + 1, HD, TILE), f32),
            pltpu.VMEM((nr, 2 * TILE, HD), f32), pltpu.VMEM((nr, 2 * TILE, HD), f32),
            pltpu.VMEM((2 * TILE, TILE), bf16), pltpu.VMEM((2 * TILE, TILE), bf16),
        ],
        compiler_params=pltpu.CompilerParams(vmem_limit_bytes=60 * 2**20),
        cost_estimate=pl.CostEstimate(flops=5 * 10**10, bytes_accessed=16 * 2**20, transcendentals=3 * 10**7),
        name="grads",
    )(tiles, q, do, k, v, z, aux_r, aux_k)


MESH = pl.DeviceIdType.MESH
HEADS, INNER, OUTER, BLK, CTX_ROWS = 8, 4, 4, 128, 1024


def peers():
    head, inner, outer = (lax.axis_index(a) for a in ("head", "inner", "outer"))
    y_peer = lax.rem(inner + 2, INNER)
    core_peer = inner + 1 - 2 * lax.rem(inner, 2)
    x_next, x_prev = lax.rem(outer + 1, OUTER), lax.rem(outer + OUTER - 1, OUTER)
    return head, inner, outer, y_peer, core_peer, x_next, x_prev


def neighbours():
    head, inner, outer, y_peer, core_peer, x_next, x_prev = peers()
    across = (1 - head // 4) * 4
    return ([{"head": lax.rem(head + j, HEADS)} for j in range(1, HEADS)]
            + [{"head": across + z, "inner": y_peer} for z in range(4)]
            + [{"inner": y_peer}, {"inner": core_peer}, {"outer": x_next}, {"outer": x_prev}])


def greet(devices):
    barrier = pltpu.get_barrier_semaphore()
    for device in devices:
        pl.semaphore_signal(barrier, inc=1, device_id=device, device_id_type=MESH)
    pl.semaphore_wait(barrier, len(devices))


def rows_at(ref, block, chunk):
    return ref.at[pl.ds(pl.multiple_of(block * CTX_ROWS + chunk * BLK, BLK), BLK)]


def spread_kernel(q, do, k, v, out, pos, q_all, do_all, k_all, v_all, aux_r, aux_k, z_ref,
                  aux, send1, recv1, send2, recv2, own_sem):
    head, inner, outer, y_peer, core_peer, x_next, x_prev = peers()
    greet(neighbours())

    def aux_at(ref, block, chunk):
        return ref.at[block, chunk]

    def fill_aux():
        for g in range(HEADS):
            aux[g, 2:8, :] = jnp.broadcast_to(pos[...].astype(f32), (6, BLK))
            for h in range(2):
                cols = slice((2 * g + h) * HD, (2 * g + h + 1) * HD)
                product = do[:, cols].astype(f32) * out[:, cols].astype(f32)
                aux[g, h:h + 1, :] = jnp.sum(product.T, axis=0, keepdims=True)

    def near(chunk):
        return chunk // 4 == head // 4

    def via(t, dest):
        if t in (0, 1, 4):
            return {"head": dest, "inner": jnp.where(near(dest), inner, y_peer)}
        return {"head": dest}

    def first(t, dest, source_head):
        if t == 4:
            return aux.at[dest], aux_at(aux_r, inner, source_head)
        if t == 5:
            return aux.at[dest], aux_at(aux_k, outer, source_head)
        src = (q, do, k, v)[t]
        dst = (q_all, do_all, k_all, v_all)[t]
        wide = 256 if t < 2 else 128
        return (src.at[:, pl.ds(pl.multiple_of(dest * wide, wide), wide)],
                rows_at(dst, inner if t < 2 else outer, source_head))

    def remote(src, dst, ssem, rsem, device):
        return pltpu.make_async_remote_copy(src_ref=src, dst_ref=dst, send_sem=ssem, recv_sem=rsem,
                                            device_id=device, device_id_type=MESH)

    ORDER = (0, 2, 4, 5, 3, 1)
    def send_part(part):
        for t in part:
            src, dst = first(t, head, head)
            pltpu.make_async_copy(src, dst, own_sem.at[t]).start()

        def send_first(j, _):
            dest = lax.rem(head + j, HEADS)
            for t in part:
                src, dst = first(t, dest, head)
                remote(src, dst, send1.at[t, dest], recv1.at[t, head], via(t, dest)).start()
            return 0

        lax.fori_loop(1, HEADS, send_first, 0)

    EARLY, LATE = (0, 2, 4, 5), (1, 3)
    send_part((0, 2))
    fill_aux()
    send_part((4, 5))
    send_part(LATE)

    def wait_own(part):
        for t in part:
            src, dst = first(t, head, head)
            pltpu.make_async_copy(src, dst, own_sem.at[t]).wait()

    wait_own(EARLY)

    y_core = lax.rem(core_peer + 2, INNER)
    x_far = lax.rem(outer + 2, OUTER)

    def base(g):
        return 4 * (head // 4) if g == 0 else 4 * (1 - head // 4)

    def piece(t, block, g):
        if t >= 4:
            return (aux_r, aux_k)[t - 4].at[block, pl.ds(base(g), 4)]
        return (q_all, do_all, k_all, v_all)[t].at[pl.ds(pl.multiple_of(block * CTX_ROWS + base(g) * BLK, 4 * BLK), 4 * BLK)]

    ROWS, KEYS = (0, 4, 1), (2, 5, 3)

    def hop(route, t, block, g, device):
        ref = piece(t, block, g)
        s = (ROWS if t in ROWS else KEYS).index(t)
        return remote(ref, ref, send2.at[route, s, g], recv2.at[route, s, g], device)

    Y, C, XN, XP = {"inner": y_peer}, {"inner": core_peer}, {"outer": x_next}, {"outer": x_prev}

    def forward(part, g):
        def wait_first(chunk):
            for t in part:
                src, dst = first(t, head, chunk)
                remote(src, dst, send1.at[t, chunk], recv1.at[t, chunk], {"head": chunk}).wait_recv()

        for n in range(4):
            chunk = base(g) + lax.rem(head + 4 - n, 4)
            if g == 1 or n > 0:
                wait_first(chunk)
        for t in part:
            if t in ROWS:
                block = inner if g == 0 else y_peer
                hop(0, t, block, g, Y).start()
                hop(1, t, block, g, C).start()
            else:
                hop(3, t, outer, g, XN).start()
                hop(4, t, outer, g, XP).start()

    def relay(part, g):
        for t in part:
            if t in ROWS:
                block = y_peer if g == 0 else inner
                hop(0, t, block, g, Y).wait_recv()
                hop(2, t, block, g, C).start()
        for t in part:
            if t in KEYS:
                hop(3, t, x_prev, g, XN).wait_recv()
                hop(4, t, x_next, g, XP).wait_recv()
                if g == 0:
                    hop(5, t, x_prev, g, XN).start()
                else:
                    hop(5, t, x_next, g, XP).start()

    def arrive(part):
        for g in range(2):
            for t in part:
                if t in ROWS:
                    hop(1, t, core_peer, g, C).wait_recv()
                    hop(2, t, y_core, g, C).wait_recv()
                else:
                    hop(5, t, x_far, g, XN).wait_recv()

    def tile(n):
        r, c = n // 4, lax.rem(n, 4)
        live = widen(column(place_of(aux_k, 2 * c))) <= place_of(aux_r, 2 * r + 1)
        kk = k_all[pl.ds(pl.multiple_of(c * CTX_ROWS, CTX_ROWS), TILE), :]
        rows = pl.ds(pl.multiple_of(r * CTX_ROWS + TILE, TILE), TILE)
        for h in range(2):
            e = jnp.exp2(jnp.tanh(nt(kk, q_all[rows, h * HD:(h + 1) * HD]) * SCALE) * CAP2)
            z_ref[r, h] += jnp.sum(jnp.where(live, e, 0.0).reshape(TILE // 8, 8, TILE), axis=0)

    def some_tiles(start, stop):
        def step(n, _):
            tile(n)
            return 0
        lax.fori_loop(start, stop, step, 0)

    forward(EARLY, 0)
    forward(EARLY, 1)
    z_ref[...] = jnp.zeros_like(z_ref)
    wait_own(LATE)
    relay(EARLY, 0)
    forward(LATE, 0)
    relay(EARLY, 1)
    forward(LATE, 1)
    arrive(EARLY)
    some_tiles(0, 2)
    relay(LATE, 0)
    some_tiles(2, 7)
    relay(LATE, 1)
    some_tiles(7, 16)
    arrive(LATE)

    for g in range(2):
        for t in ROWS:
            hop(0, t, inner, g, Y).wait_send()
            hop(1, t, inner, g, C).wait_send()
            hop(2, t, y_peer, g, C).wait_send()
        for t in KEYS:
            hop(3, t, outer, g, XN).wait_send()
            hop(4, t, outer, g, XP).wait_send()
            hop(5, t, x_prev, g, XN).wait_send()

    def finish(j, _):
        chunk = lax.rem(head + HEADS - j, HEADS)
        for t in ORDER:
            src, dst = first(t, chunk, head)
            remote(src, dst, send1.at[t, chunk], recv1.at[t, chunk], {"head": chunk}).wait_send()
        return 0

    lax.fori_loop(1, HEADS, finish, 0)


def spread(q, do, k, v, out, pos):
    hbm = pl.BlockSpec(memory_space=pl.ANY)
    vm = pl.BlockSpec(memory_space=pltpu.VMEM)
    rows = INNER * CTX_ROWS
    return pl.pallas_call(
        spread_kernel,
        out_shape=(jax.ShapeDtypeStruct((rows, 256), bf16), jax.ShapeDtypeStruct((rows, 256), bf16),
                   jax.ShapeDtypeStruct((rows, 128), bf16), jax.ShapeDtypeStruct((rows, 128), bf16),
                   jax.ShapeDtypeStruct((INNER, HEADS, 8, 128), f32), jax.ShapeDtypeStruct((OUTER, HEADS, 8, 128), f32),
                   jax.ShapeDtypeStruct((INNER, 2, 8, TILE), f32)),
        in_specs=[vm] * 6,
        out_specs=(vm, hbm, vm, hbm, vm, vm, vm),
        scratch_shapes=[pltpu.VMEM((HEADS, 8, 128), f32),
                        pltpu.SemaphoreType.DMA((6, HEADS)), pltpu.SemaphoreType.DMA((6, HEADS)),
                        pltpu.SemaphoreType.DMA((6, 3, 2)), pltpu.SemaphoreType.DMA((6, 3, 2)),
                        pltpu.SemaphoreType.DMA((6,))],
        compiler_params=pltpu.CompilerParams(collective_id=0, has_side_effects=True, vmem_limit_bytes=60 * 2**20),
        name="spread",
    )(q, do, k, v, out, pos)


def pool_kernel(z, out, recv, send_sem, recv_sem):
    head, inner, outer, y_peer, core_peer, x_next, x_prev = peers()
    others = [lax.rem(inner + j, INNER) for j in range(1, INNER)]
    greet([{"inner": o} for o in others])
    out[...] = jnp.sum(z[...], axis=2)
    copies = []
    for j, o in enumerate(others):
        copies.append(pltpu.make_async_remote_copy(
            src_ref=out, dst_ref=recv.at[j], send_sem=send_sem.at[j], recv_sem=recv_sem.at[j],
            device_id={"inner": o}, device_id_type=MESH))
        copies[-1].start()
    for c in copies:
        c.wait()
    total = jnp.zeros(out.shape, f32)
    for i in range(INNER):
        d = lax.rem(inner - i + INNER, INNER)
        part = jnp.where(d == 0, out[...], jnp.where(d == 1, recv[0], jnp.where(d == 2, recv[1], recv[2])))
        total = total + part
    out[...] = total


def pool(z):
    vm = pl.BlockSpec(memory_space=pltpu.VMEM)
    small = (z.shape[0], 2, z.shape[3])
    return pl.pallas_call(
        pool_kernel,
        out_shape=jax.ShapeDtypeStruct(small, f32),
        in_specs=[vm], out_specs=vm,
        scratch_shapes=[pltpu.VMEM((3,) + small, f32), pltpu.SemaphoreType.DMA((3,)), pltpu.SemaphoreType.DMA((3,))],
        compiler_params=pltpu.CompilerParams(collective_id=1, has_side_effects=True),
        name="pool",
    )(z)


def collect_kernel(dq, dk, dv, gq, gk, gv, q_near, kv_near, dq_pair, dq_sum, dq_far, kv_far, kv_relay, kv_sum,
                   low_q, low_k, low_v, send_sem, recv_sem, send_out, recv_out, own_sem):
    head, inner, outer, y_peer, core_peer, x_next, x_prev = peers()
    x_far = lax.rem(outer + 2, OUTER)

    def block_rows(block):
        return pl.ds(pl.multiple_of(block * CTX_ROWS, CTX_ROWS), CTX_ROWS)

    held = [pltpu.make_async_copy(dq.at[block_rows(y_peer)], q_near.at[1], own_sem.at[0]),
            pltpu.make_async_copy(dq.at[block_rows(inner)], q_near.at[0], own_sem.at[1])]
    for t in range(2):
        for x, block in enumerate((x_next, x_prev, outer)):
            held.append(pltpu.make_async_copy((dk, dv)[t].at[block_rows(block)], kv_near.at[t, x], own_sem.at[2 + 3 * t + x]))
    for copy in held:
        copy.start()
    greet(neighbours())
    y_core = lax.rem(core_peer + 2, INNER)
    Y, C, XN, XP = {"inner": y_peer}, {"inner": core_peer}, {"outer": x_next}, {"outer": x_prev}

    def remote(src, dst, ssem, rsem, device):
        return pltpu.make_async_remote_copy(src_ref=src, dst_ref=dst, send_sem=ssem, recv_sem=rsem,
                                            device_id=device, device_id_type=MESH)

    def local_rows(chunk):
        return pl.ds(pl.multiple_of(chunk * BLK, BLK), BLK)

    def near(chunk):
        return chunk // 4 == head // 4

    def pair_copy(which, chunk):
        block = jnp.where(near(chunk), *((core_peer, y_core) if which == 0 else (y_core, core_peer)))
        return remote(rows_at(dq, block, chunk), dq_pair.at[which, local_rows(chunk)],
                      send_sem.at[which, chunk], recv_sem.at[which, chunk], C)

    def far_copy(chunk):
        return remote(dq_sum.at[local_rows(chunk)], dq_far.at[local_rows(chunk)],
                      send_sem.at[2, chunk], recv_sem.at[2, chunk], Y)

    def kv_copy(t, x, chunk, device, summed=False):
        n = 3 + 3 * t + x
        src = kv_sum.at[t, local_rows(chunk)] if summed else rows_at((dk, dv)[t], (x_next, x_prev, x_far)[x], chunk)
        dst = kv_relay.at[t, local_rows(chunk)] if x == 2 else kv_far.at[t, x, local_rows(chunk)]
        return remote(src, dst, send_sem.at[n, chunk], recv_sem.at[n, chunk], device)

    def out_copy(t, chunk):
        low, out, wide = ((low_q, gq, 256), (low_k, gk, 128), (low_v, gv, 128))[t]
        device = {"head": chunk, "inner": jnp.where(near(chunk), inner, y_peer)} if t == 0 else {"head": chunk}
        return remote(low.at[local_rows(chunk)], out.at[:, pl.ds(pl.multiple_of(head * wide, wide), wide)],
                      send_out.at[t, chunk], recv_out.at[t, head], device)

    def chunk_at(j):
        return lax.rem(head + 1 + j, HEADS)

    def each_chunk(fn):
        def step(j, _):
            fn(j, chunk_at(j))
            return 0
        lax.fori_loop(0, HEADS, step, 0)

    def by_parity(chunk, even, odd):
        pl.when(lax.rem(chunk, 2) == 0)(lambda: [even(t) for t in range(2)] and None)
        pl.when(lax.rem(chunk, 2) == 1)(lambda: [odd(t) for t in range(2)] and None)

    def send_through(j, chunk):
        pair_copy(1, chunk).start()
        by_parity(chunk, lambda t: kv_copy(t, 2, chunk, XN).start(), lambda t: kv_copy(t, 2, chunk, XP).start())

    def send_direct(j, chunk):
        pair_copy(0, chunk).start()
        by_parity(chunk, lambda t: kv_copy(t, 1, chunk, XP).start(), lambda t: kv_copy(t, 0, chunk, XN).start())

    each_chunk(send_through)
    each_chunk(send_direct)
    for copy in held:
        copy.wait()

    def sum_pair(j, chunk):
        rows = local_rows(chunk)
        pair_copy(1, chunk).wait_recv()
        mine = jnp.where(near(chunk), 0, 1)
        dq_sum[rows, :] = (q_near[1 - mine, rows, :].astype(f32) + dq_pair[1, rows, :].astype(f32)).astype(bf16)
        far_copy(chunk).start()

    def sum_relay(j, chunk):
        rows = local_rows(chunk)
        odd = lax.rem(chunk, 2)
        for t in range(2):
            kv_copy(t, 2, chunk, XN).wait_recv()
            kv_sum[t, rows, :] = (kv_near[t, odd, rows, :].astype(f32) + kv_relay[t, rows, :].astype(f32)).astype(bf16)
        by_parity(chunk, lambda t: kv_copy(t, 0, chunk, XN, True).start(), lambda t: kv_copy(t, 1, chunk, XP, True).start())

    each_chunk(sum_pair)
    each_chunk(sum_relay)

    def finish_rows(j, chunk):
        rows = local_rows(chunk)
        pair_copy(0, chunk).wait_recv()
        far_copy(chunk).wait_recv()
        mine = jnp.where(near(chunk), 0, 1)
        low_q[rows, :] = (q_near[mine, rows, :].astype(f32) + dq_pair[0, rows, :].astype(f32)
                          + dq_far[rows, :].astype(f32)).astype(bf16)
        pl.when(j < HEADS - 1)(lambda: out_copy(0, chunk).start())

    def finish_keys(j, chunk):
        rows = local_rows(chunk)
        for t in range(2):
            total = kv_near[t, 2, rows, :].astype(f32)
            for x in range(2):
                kv_copy(t, x, chunk, XN).wait_recv()
                total = total + kv_far[t, x, rows, :].astype(f32)
            (low_k, low_v)[t][rows, :] = total.astype(bf16)

        @pl.when(j < HEADS - 1)
        def _():
            for t in (1, 2):
                out_copy(t, chunk).start()

    def finish_both(j, chunk):
        finish_rows(j, chunk)
        finish_keys(j, chunk)

    each_chunk(finish_both)
    own = []
    for t in range(3):
        low, out, wide = ((low_q, gq, 256), (low_k, gk, 128), (low_v, gv, 128))[t]
        own.append(pltpu.make_async_copy(low.at[local_rows(head)],
                                         out.at[:, pl.ds(pl.multiple_of(head * wide, wide), wide)], own_sem.at[t]))
        own[-1].start()

    def finish(j, _):
        chunk = chunk_at(j)
        for which in range(2):
            pair_copy(which, chunk).wait_send()
        far_copy(chunk).wait_send()
        for t in range(2):
            for x in range(3):
                kv_copy(t, x, chunk, XN).wait_send()

        @pl.when(j < HEADS - 1)
        def _():
            for t in range(3):
                low, out, wide = ((low_q, gq, 256), (low_k, gk, 128), (low_v, gv, 128))[t]
                out_copy(t, chunk).wait_send()
                remote(low.at[local_rows(head)], out.at[:, pl.ds(pl.multiple_of(chunk * wide, wide), wide)],
                       send_out.at[t, head], recv_out.at[t, chunk], {"head": chunk}).wait_recv()
        return 0

    lax.fori_loop(0, HEADS, finish, 0)
    for copy in own:
        copy.wait()


def collect(dq, dk, dv):
    hbm = pl.BlockSpec(memory_space=pl.ANY)
    wide, narrow = (CTX_ROWS, 256), (CTX_ROWS, 128)
    return pl.pallas_call(
        collect_kernel,
        out_shape=(jax.ShapeDtypeStruct((BLK, 2048), bf16), jax.ShapeDtypeStruct((BLK, 1024), bf16),
                   jax.ShapeDtypeStruct((BLK, 1024), bf16)),
        in_specs=[hbm] * 3,
        out_specs=(hbm,) * 3,
        scratch_shapes=[pltpu.VMEM((2,) + wide, bf16), pltpu.VMEM((2, 3) + narrow, bf16),
                        pltpu.VMEM((2,) + wide, bf16), pltpu.VMEM(wide, bf16), pltpu.VMEM(wide, bf16),
                        pltpu.VMEM((2, 2) + narrow, bf16), pltpu.VMEM((2,) + narrow, bf16), pltpu.VMEM((2,) + narrow, bf16),
                        pltpu.VMEM(wide, bf16), pltpu.VMEM(narrow, bf16), pltpu.VMEM(narrow, bf16),
                        pltpu.SemaphoreType.DMA((9, HEADS)), pltpu.SemaphoreType.DMA((9, HEADS)),
                        pltpu.SemaphoreType.DMA((3, HEADS)), pltpu.SemaphoreType.DMA((3, HEADS)),
                        pltpu.SemaphoreType.DMA((8,))],
        compiler_params=pltpu.CompilerParams(collective_id=2, has_side_effects=True, vmem_limit_bytes=60 * 2**20),
        name="collect",
    )(dq, dk, dv)


def hand_over_kernel(a, b, c, x, y, z):
    x[...] = a[...]
    y[...] = b[...]
    z[...] = c[...]


def hand_over(*arrays):
    vm = pl.BlockSpec(memory_space=pltpu.VMEM)
    return pl.pallas_call(
        hand_over_kernel,
        out_shape=tuple(jax.ShapeDtypeStruct(a.shape, a.dtype) for a in arrays),
        in_specs=[vm] * 3, out_specs=(vm,) * 3,
        compiler_params=pltpu.CompilerParams(vmem_limit_bytes=60 * 2**20),
        name="hand_over",
    )(*arrays)


def local(queries, keys, values, output, grad_output, positions):
    q, do, k, v, aux_r, aux_k, part = spread(queries, grad_output, keys, values, output, positions.reshape(1, BLK))
    z, tiles = totals(q, k, aux_r, aux_k, part)
    dq, dk, dv = grads(tiles, q, do, k, v, pool(z), aux_r, aux_k)
    return hand_over(*collect(dq, dk, dv))


def solution(mesh):
    rows = P(("head", "inner", "outer"), None)
    return jax.shard_map(
        local, mesh=mesh,
        in_specs=(rows,) * 5 + (P(("head", "inner", "outer")),),
        out_specs=(rows,) * 3,
        check_vma=False,
    )
```
